32 devices in a mesh: seq: 4 (over y, x), dp: 8 (over z, core).
Axes of the slice: x: 2, y: 2, z: 4, core: 2. Of those that a mesh axis runs over, the one named last changes fastest.
Arguments:
- tokens_in: bfloat16 [8, 2048, 1024], P('dp', 'seq'), may hold values from -8 to 8, as said below
- out_grad: bfloat16 [8, 2048, 1024], P('dp', 'seq'), may hold values from -6 to 6
- first_gain: bfloat16 [1024], P(('seq', 'dp')), may hold values from 0.25 to 1.75
- first_shift: bfloat16 [1024], P(('seq', 'dp')), may hold values from -1.75 to 1.75
- input_weight: bfloat16 [1024, 3072], P(('seq', 'dp')), may hold values from -0.1875 to 0.1875
- input_bias: bfloat16 [2048], P(('seq', 'dp')), may hold values from -3 to 3
- output_weight: bfloat16 [1024, 1024], P(('seq', 'dp')), may hold values from -0.75 to 0.75
- output_bias: bfloat16 [1024], P(('seq', 'dp')), may hold values from -3 to 3
- second_gain: bfloat16 [1024], P(('seq', 'dp')), may hold values from 0.25 to 1.75
- second_shift: bfloat16 [1024], P(('seq', 'dp')), may hold values from -1.75 to 1.75
- up_weight: bfloat16 [1024, 4096], P(('seq', 'dp')), may hold values from -0.1875 to 0.1875
- up_bias: bfloat16 [4096], P(('seq', 'dp')), may hold values from -3 to 3
- down_weight: bfloat16 [4096, 1024], P(('seq', 'dp')), may hold values from -0.09375 to 0.09375
- down_bias: bfloat16 [1024], P(('seq', 'dp')), may hold values from -3 to 3
Outputs:
- layer_out: bfloat16 [8, 2048, 1024], P('dp', 'seq')
- tokens_grad: float32 [8, 2048, 1024], P('dp', 'seq')
- grad_first_gain: float32 [1024], P(('seq', 'dp'))
- grad_first_shift: float32 [1024], P(('seq', 'dp'))
- grad_input_weight: float32 [1024, 3072], P(('seq', 'dp'))
- grad_input_bias: float32 [2048], P(('seq', 'dp'))
- grad_output_weight: float32 [1024, 1024], P(('seq', 'dp'))
- grad_output_bias: float32 [1024], P(('seq', 'dp'))
- grad_second_gain: float32 [1024], P(('seq', 'dp'))
- grad_second_shift: float32 [1024], P(('seq', 'dp'))
- grad_up_weight: float32 [1024, 4096], P(('seq', 'dp'))
- grad_up_bias: float32 [4096], P(('seq', 'dp'))
- grad_down_weight: float32 [4096, 1024], P(('seq', 'dp'))
- grad_down_bias: float32 [1024], P(('seq', 'dp'))
The draws below stay inside these ranges and needn't reach their ends.
Inputs may be any that keep to these rules, and one draw needn't show every extreme that they name: `tokens_in`: the block's.
All inputs are finite; a program needn't handle non-finite values.
Results may differ from the reference program's by a relative error of at most 0.0082.
Values may be sent and summed in bfloat16 or wider, within the bound.
No kernel may reach another device: no remote copies, remote signals or barrier semaphores. Data moves between devices by JAX's collectives and lax.ppermute only.
A program may use at most 192 MiB of HBM per device.

```python
import jax
import jax.numpy as jnp
from jax import lax

D = 1024
HEADS = 16
HEAD = 64
FF = 4096
LENGTH = 2048
SEQUENCES = 8


def draw_tokens_in(key, part):
    key = jax.random.fold_in(key, 11)
    rough_key, common_key = jax.random.split(key)
    region_count = 8
    region_rows = LENGTH // region_count
    rough = jax.random.normal(rough_key, (SEQUENCES, LENGTH, D), jnp.float32)
    common = jax.random.normal(common_key, (SEQUENCES, region_count, 1, D), jnp.float32)
    common = jnp.broadcast_to(common, (SEQUENCES, region_count, region_rows, D)).reshape(SEQUENCES, LENGTH, D)
    return jnp.clip(rough + common, -8.0, 8.0).astype(jnp.bfloat16)


def levels(rng, shape, pieces, least, largest):
    level = 1.0
    for position, blocks in pieces:
        steps = jax.random.uniform(jax.random.fold_in(jax.random.fold_in(rng, 6), position), (blocks,), jnp.float32, least / len(pieces), largest / len(pieces))
        level = level * jnp.repeat(jnp.exp(steps), shape[position] // blocks).reshape((-1,) + (1,) * (len(shape) - 1 - position))
    return level


def bell_draw(key, extent, scale, most, cuts=(), held_as=jnp.bfloat16):
    values = jax.random.normal(key, extent, jnp.float32) * scale
    if len(cuts) > 0:
        values = levels(key, extent, cuts, -0.22, 0.18) * values
    return jnp.clip(values, min=-most, max=most).astype(held_as)


def setup_inputs(seed: int = 0) -> dict:
    seeds = jax.random.split(jax.random.key(seed), 15)
    return {
        "tokens_in": draw_tokens_in(jax.random.fold_in(seeds[14], 71), 0),
        "out_grad": bell_draw(seeds[1], (SEQUENCES, LENGTH, D), 1.0, 6.0, ((0, 8), (1, 4))),
        "first_gain": jnp.clip(1.0 + 0.15 * jax.random.normal(seeds[2], (D,), jnp.float32), 0.25, 1.75).astype(jnp.bfloat16),
        "first_shift": bell_draw(seeds[3], (D,), 0.3, 1.75, ((0, 32),)),
        "input_weight": bell_draw(seeds[4], (D, 3 * D), D ** -0.5, 0.1875, ((0, 32),)),
        "input_bias": bell_draw(seeds[5], (2 * D,), 0.5, 3.0, ((0, 32),)),
        "output_weight": bell_draw(seeds[6], (D, D), (D // 16) ** -0.5, 0.75, ((0, 32),)),
        "output_bias": bell_draw(seeds[7], (D,), 0.5, 3.0, ((0, 32),)),
        "second_gain": jnp.clip(1.0 + 0.15 * jax.random.normal(seeds[8], (D,), jnp.float32), 0.25, 1.75).astype(jnp.bfloat16),
        "second_shift": bell_draw(seeds[9], (D,), 0.3, 1.75, ((0, 32),)),
        "up_weight": bell_draw(seeds[10], (D, FF), D ** -0.5, 0.1875, ((0, 32),)),
        "up_bias": bell_draw(seeds[11], (FF,), 0.5, 3.0, ((0, 32),)),
        "down_weight": bell_draw(seeds[12], (FF, D), FF ** -0.5, 0.09375, ((0, 32),)),
        "down_bias": bell_draw(seeds[13], (D,), 0.5, 3.0, ((0, 32),)),
    }


@jax.custom_vjp
def low(v):
    return lax.optimization_barrier(v.astype(jnp.bfloat16)).astype(jnp.float32)

@jax.custom_vjp
def low_back(v):
    return v

def low_keep(v):
    return (low(v), None)

def low_pass(kept, grad):
    return (grad,)

def back_keep(v):
    return (v, None)

def back_low(kept, grad):
    return (low(grad),)
low.defvjp(low_keep, low_pass)
low_back.defvjp(back_keep, back_low)
EPSILON = 1e-05
HIGHEST = lax.Precision.HIGHEST

def layer_norm(values, norm_gain, norm_shift):
    centre = values - lax.optimization_barrier(jnp.mean(values, axis=-1, keepdims=True))
    spread = lax.optimization_barrier(jnp.mean(centre * centre, axis=-1, keepdims=True))
    return centre * lax.rsqrt(spread + EPSILON) * norm_gain + norm_shift

def attend(query_rows, key_rows, value_rows, row_start, slopes):
    raw_scores = jnp.einsum('qhe,khe->hqk', query_rows, key_rows, precision=HIGHEST)
    row_place = row_start + jnp.arange(query_rows.shape[0], dtype=jnp.int32)
    col_place = jnp.arange(key_rows.shape[0], dtype=jnp.int32)
    offset = (row_place[:, None] - col_place[None, :]).astype(jnp.float32)
    scores = low_back(raw_scores) * HEAD ** (-0.5) - slopes[:, None, None] * offset
    scores = jnp.where(offset >= 0, scores, -jnp.inf)
    soft_probs = jax.nn.softmax(scores, axis=-1)
    return jnp.einsum('hqk,khe->qhe', low(soft_probs), value_rows, precision=HIGHEST)

def one_sequence(seq_rows, params):
    first_gain, first_shift, input_weight, input_bias, output_weight, output_bias, second_gain, second_shift, up_weight, up_bias, down_weight, down_bias = params
    normed = low(layer_norm(seq_rows, first_gain, first_shift))
    projected = jnp.dot(normed, input_weight, precision=HIGHEST)
    queries = low_back(low(projected[:, :D] + input_bias[:D]))
    key_rows = low_back(low(projected[:, D:2 * D]))
    value_rows = low_back(low(projected[:, 2 * D:] + input_bias[D:]))
    block_rows = min(512, LENGTH)
    block_count = LENGTH // block_rows
    head_ids = jnp.arange(HEADS, dtype=jnp.int32).astype(jnp.float32)
    slopes = jnp.exp2(-8.0 * (head_ids + 1.0) / HEADS)
    key_heads = key_rows.reshape(LENGTH, HEADS, HEAD)
    value_heads = value_rows.reshape(LENGTH, HEADS, HEAD)
    query_blocks = queries.reshape(block_count, block_rows, HEADS, HEAD)
    block_starts = jnp.arange(block_count, dtype=jnp.int32) * block_rows

    def one_block(block_pair):
        return attend(block_pair[0], key_heads, value_heads, block_pair[1], slopes)
    attended = lax.map(jax.checkpoint(one_block), (query_blocks, block_starts))
    context = low_back(low(attended.reshape(LENGTH, D)))
    branch = low_back(jnp.dot(context, output_weight, precision=HIGHEST)) + output_bias
    residual = seq_rows + branch
    normed_two = low(layer_norm(residual, second_gain, second_shift))
    upper = low_back(jnp.dot(normed_two, up_weight, precision=HIGHEST)) + up_bias
    hidden = low(jax.nn.gelu(upper, approximate=True))
    return residual + jnp.dot(hidden, down_weight, precision=HIGHEST) + down_bias

def forward(all_rows, params):

    def per_sequence(seq_rows):
        return one_sequence(seq_rows, params)
    return lax.map(jax.checkpoint(per_sequence), all_rows)

def reference(tokens_in, out_grad, first_gain, first_shift, input_weight, input_bias, output_weight, output_bias, second_gain, second_shift, up_weight, up_bias, down_weight, down_bias):
    params = (first_gain.astype(jnp.float32), first_shift.astype(jnp.float32), input_weight.astype(jnp.float32), input_bias.astype(jnp.float32), output_weight.astype(jnp.float32), output_bias.astype(jnp.float32), second_gain.astype(jnp.float32), second_shift.astype(jnp.float32), up_weight.astype(jnp.float32), up_bias.astype(jnp.float32), down_weight.astype(jnp.float32), down_bias.astype(jnp.float32))
    outputs, backward = jax.vjp(forward, tokens_in.astype(jnp.float32), params)
    tokens_grad, grads = backward(out_grad.astype(jnp.float32))
    return (outputs.astype(jnp.bfloat16), tokens_grad, grads[0], grads[1], grads[2], grads[3], grads[4], grads[5], grads[6], grads[7], grads[8], grads[9], grads[10], grads[11])
```

```python
import functools
import math

import jax
import jax.numpy as jnp
from jax import lax
from jax.experimental import pallas as pl
from jax.experimental.pallas import tpu as pltpu
from jax.sharding import Mesh
from jax.sharding import PartitionSpec as P

HEADS = 16
HEAD = 64
EPSILON = 1e-05
LOG2E = math.log2(math.e)
TILE = 256
VMEM_BYTES = 60 * 1024 * 1024
CORES = 2
CHIPS = ("seq", "ring")
WORLD = ("seq", "ring", "core")

def _dot(a, b):
    return jnp.dot(a, b, preferred_element_type=jnp.float32)

def _bias_tile(slope):
    return lax.broadcasted_iota(jnp.int32, (TILE, TILE), 0).astype(jnp.float32) * slope

def _keep():
    return lax.broadcasted_iota(jnp.int32, (TILE, TILE), 0) <= lax.broadcasted_iota(jnp.int32, (TILE, TILE), 1)

def _row_mask(shape, axis, half):
    ids = lax.broadcasted_iota(jnp.int32, shape, axis)
    return (ids >= HEAD) == (half == 1)

def forward_kernel(slope_ref, q_ref, k_ref, v_ref, ctx_ref, wide_ref, log_ref, q_turn, v_turn, scores):
    head = pl.program_id(0)
    half = lax.rem(head, 2)
    length = q_ref.shape[0]
    tiles = length // TILE

    @pl.when(half == 0)
    def _():
        q_turn[...] = q_ref[...].T
        v_turn[...] = v_ref[...].T

    slope = slope_ref[head] * LOG2E
    scale = HEAD ** -0.5 * LOG2E
    rows = pl.ds(pl.multiple_of(half * HEAD, HEAD), HEAD)
    bias = _bias_tile(slope)
    for i in range(tiles):
        cols = slice(i * TILE, (i + 1) * TILE)
        q_block = q_turn[:, cols]
        q_block = jnp.where(_row_mask(q_block.shape, 0, half), q_block, jnp.zeros_like(q_block))
        peak = None
        for c in range(i + 1):
            part = _dot(k_ref[c * TILE:(c + 1) * TILE, :], q_block) * scale + bias
            if c == i:
                part = jnp.where(_keep(), part, -jnp.inf)
            scores[i % 2, c] = part
            top = jnp.max(part, axis=0, keepdims=True) + slope * ((c - i) * TILE)
            peak = top if peak is None else jnp.maximum(peak, top)
        total = jnp.zeros((1, TILE), jnp.float32)
        out = jnp.zeros((HEAD, TILE), jnp.float32)
        for c in range(i + 1):
            probs = jnp.exp2(scores[i % 2, c] - (peak - slope * ((c - i) * TILE)))
            total = total + jnp.sum(probs, axis=0, keepdims=True)
            out = out + _dot(v_turn[rows, c * TILE:(c + 1) * TILE], probs.astype(jnp.bfloat16))
        wide_ref[rows, cols] = out / total
        log_ref[:, cols] = jnp.broadcast_to(peak + jnp.log2(total), (8, TILE))

    @pl.when(half == 1)
    def _():
        ctx_ref[...] = wide_ref[...].T.astype(jnp.bfloat16)

def attend_forward(slopes, qkv):
    length, triple = qkv.shape
    heads = triple // (3 * HEAD)
    pairs = heads // 2
    spec = lambda part: pl.BlockSpec((length, 2 * HEAD), lambda h, part=part: (0, part * pairs + h // 2))
    return pl.pallas_call(
        forward_kernel,
        grid=(heads,),
        in_specs=[pl.BlockSpec(memory_space=pltpu.SMEM), spec(0), spec(1), spec(2)],
        out_specs=[
            pl.BlockSpec((length, 2 * HEAD), lambda h: (0, h // 2)),
            pl.BlockSpec((2 * HEAD, length), lambda h: (h // 2, 0)),
            pl.BlockSpec((8, length), lambda h: (h, 0)),
        ],
        out_shape=[
            jax.ShapeDtypeStruct((length, heads * HEAD), jnp.bfloat16),
            jax.ShapeDtypeStruct((heads * HEAD, length), jnp.float32),
            jax.ShapeDtypeStruct((heads * 8, length), jnp.float32),
        ],
        scratch_shapes=[
            pltpu.VMEM((2 * HEAD, length), jnp.bfloat16),
            pltpu.VMEM((2 * HEAD, length), jnp.bfloat16),
            pltpu.VMEM((2, length // TILE, TILE, TILE), jnp.float32),
        ],
        compiler_params=pltpu.CompilerParams(vmem_limit_bytes=VMEM_BYTES),
        name="attend_forward",
    )(slopes, qkv, qkv, qkv)

def backward_kernel(slope_ref, q_ref, k_ref, v_ref, g_ref, wide_ref, log_ref, out_ref, q_turn, k_turn, g_turn, dq_turn, dk_sum, dv_sum):
    head = pl.program_id(0)
    half = lax.rem(head, 2)
    length = q_ref.shape[0]
    tiles = length // TILE
    heads = out_ref.shape[1] // (3 * HEAD)
    wide = heads * HEAD

    @pl.when(half == 0)
    def _():
        q_turn[...] = q_ref[...].T
        k_turn[...] = k_ref[...].T
        g_turn[...] = g_ref[...].T

    slope = slope_ref[head] * LOG2E
    scale = HEAD ** -0.5 * LOG2E
    rows = pl.ds(pl.multiple_of(half * HEAD, HEAD), HEAD)
    bias = _bias_tile(slope)
    inner = jnp.sum(wide_ref[rows, :] * g_turn[rows, :].astype(jnp.float32), axis=0, keepdims=True)
    for c in range(tiles):
        span = slice(c * TILE, (c + 1) * TILE)
        dk = jnp.zeros((TILE, 2 * HEAD), jnp.float32)
        dv = jnp.zeros((TILE, 2 * HEAD), jnp.float32)
        for i in range(c, tiles):
            cols = slice(i * TILE, (i + 1) * TILE)
            q_cols = q_turn[:, cols]
            q_cols = jnp.where(_row_mask(q_cols.shape, 0, half), q_cols, jnp.zeros_like(q_cols))
            g_cols = g_turn[:, cols]
            g_cols = jnp.where(_row_mask(g_cols.shape, 0, half), g_cols, jnp.zeros_like(g_cols))
            q_rows = q_ref[cols, :]
            q_rows = jnp.where(_row_mask(q_rows.shape, 1, half), q_rows, jnp.zeros_like(q_rows))
            g_rows = g_ref[cols, :]
            g_rows = jnp.where(_row_mask(g_rows.shape, 1, half), g_rows, jnp.zeros_like(g_rows))
            part = _dot(k_ref[span, :], q_cols) * scale + bias
            if c == i:
                part = jnp.where(_keep(), part, -jnp.inf)
            probs = jnp.exp2(part - (log_ref[0:1, cols] - slope * ((c - i) * TILE)))
            grad = (probs * (_dot(v_ref[span, :], g_cols) - inner[:, cols])).astype(jnp.bfloat16)
            dv = dv + _dot(probs.astype(jnp.bfloat16), g_rows)
            dk = dk + _dot(grad, q_rows)
            dq = _dot(k_turn[rows, span], grad)
            if c == 0:
                dq_turn[rows, cols] = dq
            else:
                dq_turn[rows, cols] += dq

        @pl.when(half == 0)
        def _():
            dk_sum[span, :] = dk
            dv_sum[span, :] = dv

        @pl.when(half == 1)
        def _():
            lane = pl.multiple_of((head // 2) * 2 * HEAD, 2 * HEAD)
            out_ref[span, pl.ds(wide + lane, 2 * HEAD)] = ((dk_sum[span, :] + dk) * HEAD ** -0.5).astype(jnp.bfloat16)
            out_ref[span, pl.ds(2 * wide + lane, 2 * HEAD)] = (dv_sum[span, :] + dv).astype(jnp.bfloat16)

    @pl.when(half == 1)
    def _():
        lane = pl.multiple_of((head // 2) * 2 * HEAD, 2 * HEAD)
        out_ref[:, pl.ds(lane, 2 * HEAD)] = (dq_turn[...] * HEAD ** -0.5).T.astype(jnp.bfloat16)

def attend_backward(slopes, qkv, grad, wide, log):
    length, triple = qkv.shape
    heads = triple // (3 * HEAD)
    pairs = heads // 2
    spec = lambda part: pl.BlockSpec((length, 2 * HEAD), lambda h, part=part: (0, part * pairs + h // 2))
    return pl.pallas_call(
        backward_kernel,
        grid=(heads,),
        in_specs=[
            pl.BlockSpec(memory_space=pltpu.SMEM), spec(0), spec(1), spec(2),
            pl.BlockSpec((length, 2 * HEAD), lambda h: (0, h // 2)),
            pl.BlockSpec((2 * HEAD, length), lambda h: (h // 2, 0)),
            pl.BlockSpec((8, length), lambda h: (h, 0)),
        ],
        out_specs=pl.BlockSpec((length, triple), lambda h: (0, 0)),
        out_shape=jax.ShapeDtypeStruct((length, triple), jnp.bfloat16),
        scratch_shapes=[
            pltpu.VMEM((2 * HEAD, length), jnp.bfloat16),
            pltpu.VMEM((2 * HEAD, length), jnp.bfloat16),
            pltpu.VMEM((2 * HEAD, length), jnp.bfloat16),
            pltpu.VMEM((2 * HEAD, length), jnp.float32),
            pltpu.VMEM((length, 2 * HEAD), jnp.float32),
            pltpu.VMEM((length, 2 * HEAD), jnp.float32),
        ],
        compiler_params=pltpu.CompilerParams(vmem_limit_bytes=VMEM_BYTES),
        name="attend_backward",
    )(slopes, qkv, qkv, qkv, grad, wide, log)

def layer_norm(values, norm_gain, norm_shift):
    centre = values - jnp.mean(values, axis=-1, keepdims=True)
    spread = jnp.mean(centre * centre, axis=-1, keepdims=True)
    return centre * lax.rsqrt(spread + EPSILON) * norm_gain + norm_shift


def tanh_gelu(upper_in):
    return jax.nn.gelu(upper_in, approximate=True)


def gather_small(parts):
    sizes = [part.shape[0] for part in parts]
    width = -(-sum(sizes) // 512) * 512
    packed = jnp.concatenate(list(parts) + [jnp.zeros((width - sum(sizes),), parts[0].dtype)])
    whole = lax.all_gather(packed.reshape(4, width // 4), WORLD, axis=0, tiled=False)
    whole = whole.reshape(-1, width).astype(jnp.float32)
    out, start = [], 0
    for size in sizes:
        out.append(whole[:, start : start + size].reshape(-1))
        start += size
    return out


def scatter_small(parts, world):
    rows = [part.reshape(world, -1) for part in parts]
    sizes = [row.shape[1] for row in rows]
    width = -(-sum(sizes) // 128) * 128
    packed = jnp.concatenate(rows + [jnp.zeros((world, width - sum(sizes)), jnp.float32)], axis=1)
    owned = lax.psum_scatter(packed, WORLD, scatter_dimension=0, tiled=True)[0]
    out, start = [], 0
    for size in sizes:
        out.append(owned[start : start + size])
        start += size
    return out


def other_core(value):
    return lax.ppermute(value, "core", [(0, 1), (1, 0)])


def gather_weight(shard):
    mine = lax.all_gather(shard, CHIPS, axis=0, tiled=False)
    theirs = other_core(mine)
    first = lax.axis_index("core") == 0
    pair = jnp.stack((jnp.where(first, mine, theirs), jnp.where(first, theirs, mine)), axis=1)
    return pair.reshape(-1, shard.shape[-1])


def pick_rows(columns, chips, core):
    tokens, width = columns.shape
    parts = columns.reshape(tokens, chips, CORES, width // (chips * CORES))
    return lax.dynamic_index_in_dim(parts, core, 2, keepdims=False).reshape(tokens, width // CORES)


def contract_tokens(left, right):
    return lax.dot_general(left, right, (((0,), (0,)), ((), ())), preferred_element_type=jnp.float32)


def scatter_weight_grad(left, right, chips):
    core = lax.axis_index("core")
    sent = contract_tokens(pick_rows(left, chips, 1 - core), right).astype(jnp.bfloat16)
    came = other_core(sent).astype(jnp.float32)
    both = (contract_tokens(pick_rows(left, chips, core), right) + came).astype(jnp.bfloat16)
    return lax.psum_scatter(both, CHIPS, scatter_dimension=0, tiled=True).astype(jnp.float32)


def body(
    tokens_in,
    out_grad,
    first_gain,
    first_shift,
    input_weight,
    input_bias,
    output_weight,
    output_bias,
    second_gain,
    second_shift,
    up_weight,
    up_bias,
    down_weight,
    down_bias,
):
    ways = lax.axis_size("seq")
    rings = lax.axis_size("ring")
    chips = ways * rings
    model_width = tokens_in.shape[-1]
    group_width = model_width // ways
    head_group = group_width // HEAD
    rows_in = tokens_in.reshape(-1, model_width)
    local = rows_in.shape[0]
    length = local * ways
    upstream = out_grad.reshape(local, model_width)

    (
        gain_first,
        shift_first,
        bias_input,
        bias_output,
        gain_second,
        shift_second,
        bias_up,
        bias_down,
    ) = gather_small(
        (first_gain, first_shift, input_bias, output_bias, second_gain, second_shift, up_bias, down_bias)
    )
    seq_index = lax.axis_index("seq")

    all_rows = lax.all_gather(rows_in, "seq", axis=0, tiled=True)
    owned_rows = input_weight.shape[0]
    by_group = input_weight.reshape(owned_rows, 3, ways, group_width)
    by_group = jnp.moveaxis(by_group, 2, 0).reshape(ways, owned_rows, 3 * group_width)
    columns = lax.all_to_all(by_group, "seq", split_axis=0, concat_axis=0, tiled=True)
    columns = lax.all_gather(columns, ("ring", "core"), axis=0, tiled=False)
    weight_input = jnp.moveaxis(columns, 0, 1).reshape(model_width, 3 * group_width)

    weight_output = gather_weight(output_weight)
    weight_up = gather_weight(up_weight)
    weight_down = gather_weight(down_weight)

    normed = layer_norm(all_rows.astype(jnp.float32), gain_first, shift_first).astype(jnp.bfloat16)
    start = seq_index * group_width
    bias_group = jnp.concatenate(
        (
            lax.dynamic_slice_in_dim(bias_input, start, group_width),
            jnp.zeros((group_width,), jnp.float32),
            lax.dynamic_slice_in_dim(bias_input, model_width + start, group_width),
        )
    )
    qkv = (jnp.dot(normed, weight_input, preferred_element_type=jnp.float32) + bias_group).astype(
        jnp.bfloat16
    )
    head_ids = (seq_index * head_group + jnp.arange(head_group, dtype=jnp.int32)).astype(jnp.float32)
    slopes = jnp.exp2(-8.0 * (head_ids + 1.0) / HEADS)
    context_split, wide, log_totals = attend_forward(slopes, qkv)
    context = lax.all_to_all(
        context_split.reshape(ways, local, group_width), "seq", split_axis=0, concat_axis=0, tiled=True
    )
    context = jnp.moveaxis(context, 0, 1).reshape(local, model_width)

    inputs = rows_in.astype(jnp.float32)
    branch = jnp.dot(context, weight_output, preferred_element_type=jnp.float32) + bias_output
    residual = inputs + branch
    normed_two_float, second_back = jax.vjp(layer_norm, residual, gain_second, shift_second)
    normed_two = normed_two_float.astype(jnp.bfloat16)
    upper = jnp.dot(normed_two, weight_up, preferred_element_type=jnp.float32) + bias_up
    activated, gelu_back = jax.vjp(tanh_gelu, upper)
    hidden = activated.astype(jnp.bfloat16)
    layer_out = (
        residual + jnp.dot(hidden, weight_down, preferred_element_type=jnp.float32) + bias_down
    ).astype(jnp.bfloat16)
    grad_hidden = lax.dot_general(
        upstream, weight_down, (((1,), (1,)), ((), ())), preferred_element_type=jnp.float32
    )
    grad_upper = gelu_back(grad_hidden)[0]
    upper_low = grad_upper.astype(jnp.bfloat16)
    grad_normed_two = lax.dot_general(
        upper_low, weight_up, (((1,), (1,)), ((), ())), preferred_element_type=jnp.float32
    )
    grad_through, grad_second_gain, grad_second_shift = second_back(grad_normed_two)
    grad_residual = upstream.astype(jnp.float32) + grad_through
    branch_low = grad_residual.astype(jnp.bfloat16)
    context_grad = lax.dot_general(
        branch_low, weight_output, (((1,), (1,)), ((), ())), preferred_element_type=jnp.float32
    ).astype(jnp.bfloat16)
    grad_split = jnp.moveaxis(context_grad.reshape(local, ways, group_width), 1, 0)
    grad_split = lax.all_to_all(grad_split, "seq", split_axis=0, concat_axis=0, tiled=True)
    grad_split = grad_split.reshape(length, group_width)

    grad_down_weight = scatter_weight_grad(hidden, upstream, chips)
    grad_up_weight = scatter_weight_grad(normed_two, upper_low, chips)
    grad_output_weight = scatter_weight_grad(context, branch_low, chips)

    grad_qkv = attend_backward(slopes, qkv, grad_split, wide, log_totals)

    grad_normed = lax.dot_general(
        grad_qkv, weight_input, (((1,), (1,)), ((), ())), preferred_element_type=jnp.float32
    ).astype(jnp.bfloat16)
    grad_normed = lax.all_to_all(
        grad_normed.reshape(ways, local, model_width), "seq", split_axis=0, concat_axis=0, tiled=True
    )
    grad_normed = jnp.sum(grad_normed.astype(jnp.float32), axis=0)

    grad_columns = contract_tokens(normed, grad_qkv)
    grad_columns = jnp.moveaxis(
        grad_columns.reshape(ways, rings * CORES, owned_rows, 3 * group_width), 1, 0
    ).astype(jnp.bfloat16)
    grad_columns = lax.psum_scatter(
        grad_columns.reshape(-1, 3 * group_width), ("ring", "core"), scatter_dimension=0, tiled=True
    )
    grad_columns = lax.all_to_all(
        grad_columns.reshape(ways, owned_rows, 3 * group_width), "seq", split_axis=0, concat_axis=0, tiled=True
    )
    grad_input_weight = jnp.moveaxis(
        grad_columns.reshape(ways, owned_rows, 3, group_width), 0, 2
    ).reshape(owned_rows, 3 * model_width).astype(jnp.float32)

    bias_sums = jnp.sum(grad_qkv.astype(jnp.float32), axis=0)
    empty = jnp.zeros((2 * model_width,), jnp.float32)
    grad_input_bias = lax.dynamic_update_slice(empty, bias_sums[:group_width], (start,))
    grad_input_bias = lax.dynamic_update_slice(
        grad_input_bias, bias_sums[2 * group_width :], (model_width + start,)
    )

    _, first_back = jax.vjp(layer_norm, inputs, gain_first, shift_first)
    grad_entry, grad_first_gain, grad_first_shift = first_back(grad_normed)
    tokens_grad = grad_residual + grad_entry

    small = scatter_small(
        (
            grad_first_gain,
            grad_first_shift,
            grad_input_bias,
            jnp.sum(grad_residual, axis=0),
            grad_second_gain,
            grad_second_shift,
            jnp.sum(grad_upper, axis=0),
            jnp.sum(upstream.astype(jnp.float32), axis=0),
        ),
        chips * CORES,
    )
    return (
        layer_out.reshape(tokens_in.shape),
        tokens_grad.reshape(tokens_in.shape),
        small[0],
        small[1],
        grad_input_weight,
        small[2],
        grad_output_weight,
        small[3],
        small[4],
        small[5],
        grad_up_weight,
        small[6],
        grad_down_weight,
        small[7],
    )


def solution(mesh):
    ways, copies = mesh.shape["seq"], mesh.shape["dp"]
    split = Mesh(mesh.devices.reshape(ways, copies // CORES, CORES), WORLD)
    token = P(("ring", "core"), "seq", None)
    vector = P(WORLD)
    matrix = P(WORLD, None)
    weights = (vector, vector, matrix, vector, matrix, vector, vector, vector, matrix, vector, matrix, vector)
    return jax.shard_map(
        body,
        mesh=split,
        in_specs=(token, token) + weights,
        out_specs=(token, token) + weights,
        check_vma=False,
    )
```

```python
import functools
import math

import jax
import jax.numpy as jnp
from jax import lax
from jax.experimental import pallas as pl
from jax.experimental.pallas import tpu as pltpu
from jax.sharding import Mesh
from jax.sharding import PartitionSpec as P

HEADS = 16
HEAD = 64
EPSILON = 1e-05
LOG2E = math.log2(math.e)
TILE = 256
VMEM_BYTES = 60 * 1024 * 1024
CORES = 2
CHIPS = ("seq", "ring")
WORLD = ("seq", "ring", "core")

def _dot(a, b):
    return jnp.dot(a, b, preferred_element_type=jnp.float32)

def _bias_tile(slope):
    return lax.broadcasted_iota(jnp.int32, (TILE, TILE), 0).astype(jnp.float32) * slope

def _keep():
    return lax.broadcasted_iota(jnp.int32, (TILE, TILE), 0) <= lax.broadcasted_iota(jnp.int32, (TILE, TILE), 1)

def _row_mask(shape, axis, half):
    ids = lax.broadcasted_iota(jnp.int32, shape, axis)
    return (ids >= HEAD) == (half == 1)

def estimate(micros):
    return pl.CostEstimate(flops=int(micros * 1e8), bytes_accessed=0, transcendentals=0)

def forward_kernel(slope_ref, q_ref, k_ref, v_ref, *refs):
    ctx_ref, wide_ref, log_ref, q_turn, v_turn, scores = refs[-6:]
    head = pl.program_id(0)
    half = lax.rem(head, 2)
    length = q_ref.shape[0]
    tiles = length // TILE

    @pl.when(half == 0)
    def _():
        q_turn[...] = q_ref[...].T
        v_turn[...] = v_ref[...].T

    slope = slope_ref[head] * LOG2E
    scale = HEAD ** -0.5 * LOG2E
    rows = pl.ds(pl.multiple_of(half * HEAD, HEAD), HEAD)
    bias = _bias_tile(slope)
    for i in range(tiles):
        cols = slice(i * TILE, (i + 1) * TILE)
        q_block = q_turn[:, cols]
        q_block = jnp.where(_row_mask(q_block.shape, 0, half), q_block, jnp.zeros_like(q_block))
        peak = None
        for c in range(i + 1):
            part = _dot(k_ref[c * TILE:(c + 1) * TILE, :], q_block) * scale + bias
            if c == i:
                part = jnp.where(_keep(), part, -jnp.inf)
            scores[i % 2, c] = part
            top = jnp.max(part, axis=0, keepdims=True) + slope * ((c - i) * TILE)
            peak = top if peak is None else jnp.maximum(peak, top)
        total = jnp.zeros((1, TILE), jnp.float32)
        out = jnp.zeros((HEAD, TILE), jnp.float32)
        for c in range(i + 1):
            probs = jnp.exp2(scores[i % 2, c] - (peak - slope * ((c - i) * TILE)))
            total = total + jnp.sum(probs, axis=0, keepdims=True)
            out = out + _dot(v_turn[rows, c * TILE:(c + 1) * TILE], probs.astype(jnp.bfloat16))
        wide_ref[rows, cols] = out / total
        log_ref[:, cols] = jnp.broadcast_to(peak + jnp.log2(total), (8, TILE))

    @pl.when(half == 1)
    def _():
        ctx_ref[...] = wide_ref[...].T.astype(jnp.bfloat16)

def attend_forward(slopes, qkv, pair, deps=()):
    length = qkv.shape[0]
    spec = lambda part: pl.BlockSpec((length, 2 * HEAD), lambda h: (0, 3 * pair + part))
    return pl.pallas_call(
        forward_kernel,
        grid=(2,),
        in_specs=[pl.BlockSpec(memory_space=pltpu.SMEM), spec(0), spec(1), spec(2)]
        + [pl.BlockSpec(memory_space=pl.ANY)] * len(deps),
        out_specs=[
            pl.BlockSpec((length, 2 * HEAD), lambda h: (0, 0)),
            pl.BlockSpec((2 * HEAD, length), lambda h: (0, 0)),
            pl.BlockSpec((8, length), lambda h: (h, 0)),
        ],
        out_shape=[
            jax.ShapeDtypeStruct((length, 2 * HEAD), jnp.bfloat16),
            jax.ShapeDtypeStruct((2 * HEAD, length), jnp.float32),
            jax.ShapeDtypeStruct((2 * 8, length), jnp.float32),
        ],
        scratch_shapes=[
            pltpu.VMEM((2 * HEAD, length), jnp.bfloat16),
            pltpu.VMEM((2 * HEAD, length), jnp.bfloat16),
            pltpu.VMEM((2, length // TILE, TILE, TILE), jnp.float32),
        ],
        compiler_params=pltpu.CompilerParams(vmem_limit_bytes=VMEM_BYTES),
        cost_estimate=estimate(10.5),
        name="attend_forward",
    )(slopes, qkv, qkv, qkv, *deps)

def backward_kernel(slope_ref, q_ref, k_ref, v_ref, g_ref, wide_ref, log_ref, *refs):
    out_ref, q_turn, k_turn, g_turn, dq_turn, dk_sum, dv_sum = refs[-7:]
    head = pl.program_id(0)
    half = lax.rem(head, 2)
    length = q_ref.shape[0]
    tiles = length // TILE
    wide = 2 * HEAD

    @pl.when(half == 0)
    def _():
        q_turn[...] = q_ref[...].T
        k_turn[...] = k_ref[...].T
        g_turn[...] = g_ref[...].T

    slope = slope_ref[head] * LOG2E
    scale = HEAD ** -0.5 * LOG2E
    rows = pl.ds(pl.multiple_of(half * HEAD, HEAD), HEAD)
    bias = _bias_tile(slope)
    inner = jnp.sum(wide_ref[rows, :] * g_turn[rows, :].astype(jnp.float32), axis=0, keepdims=True)
    for c in range(tiles):
        span = slice(c * TILE, (c + 1) * TILE)
        dk = jnp.zeros((TILE, 2 * HEAD), jnp.float32)
        dv = jnp.zeros((TILE, 2 * HEAD), jnp.float32)
        for i in range(c, tiles):
            cols = slice(i * TILE, (i + 1) * TILE)
            q_cols = q_turn[:, cols]
            q_cols = jnp.where(_row_mask(q_cols.shape, 0, half), q_cols, jnp.zeros_like(q_cols))
            g_cols = g_turn[:, cols]
            g_cols = jnp.where(_row_mask(g_cols.shape, 0, half), g_cols, jnp.zeros_like(g_cols))
            q_rows = q_ref[cols, :]
            q_rows = jnp.where(_row_mask(q_rows.shape, 1, half), q_rows, jnp.zeros_like(q_rows))
            g_rows = g_ref[cols, :]
            g_rows = jnp.where(_row_mask(g_rows.shape, 1, half), g_rows, jnp.zeros_like(g_rows))
            part = _dot(k_ref[span, :], q_cols) * scale + bias
            if c == i:
                part = jnp.where(_keep(), part, -jnp.inf)
            probs = jnp.exp2(part - (log_ref[0:1, cols] - slope * ((c - i) * TILE)))
            grad = (probs * (_dot(v_ref[span, :], g_cols) - inner[:, cols])).astype(jnp.bfloat16)
            dv = dv + _dot(probs.astype(jnp.bfloat16), g_rows)
            dk = dk + _dot(grad, q_rows)
            dq = _dot(k_turn[rows, span], grad)
            if c == 0:
                dq_turn[rows, cols] = dq
            else:
                dq_turn[rows, cols] += dq

        @pl.when(half == 0)
        def _():
            dk_sum[span, :] = dk
            dv_sum[span, :] = dv

        @pl.when(half == 1)
        def _():
            out_ref[span, wide : 2 * wide] = ((dk_sum[span, :] + dk) * HEAD ** -0.5).astype(jnp.bfloat16)
            out_ref[span, 2 * wide :] = (dv_sum[span, :] + dv).astype(jnp.bfloat16)

    @pl.when(half == 1)
    def _():
        out_ref[:, :wide] = (dq_turn[...] * HEAD ** -0.5).T.astype(jnp.bfloat16)

def attend_backward(slopes, qkv, grad, wide, log, pair, deps=()):
    length = qkv.shape[0]
    spec = lambda part: pl.BlockSpec((length, 2 * HEAD), lambda h: (0, 3 * pair + part))
    return pl.pallas_call(
        backward_kernel,
        grid=(2,),
        in_specs=[
            pl.BlockSpec(memory_space=pltpu.SMEM), spec(0), spec(1), spec(2),
            pl.BlockSpec((length, 2 * HEAD), lambda h: (0, pair)),
            pl.BlockSpec((2 * HEAD, length), lambda h: (0, 0)),
            pl.BlockSpec((8, length), lambda h: (h, 0)),
        ] + [pl.BlockSpec(memory_space=pl.ANY)] * len(deps),
        out_specs=pl.BlockSpec((length, 6 * HEAD), lambda h: (0, 0)),
        out_shape=jax.ShapeDtypeStruct((length, 6 * HEAD), jnp.bfloat16),
        scratch_shapes=[
            pltpu.VMEM((2 * HEAD, length), jnp.bfloat16),
            pltpu.VMEM((2 * HEAD, length), jnp.bfloat16),
            pltpu.VMEM((2 * HEAD, length), jnp.bfloat16),
            pltpu.VMEM((2 * HEAD, length), jnp.float32),
            pltpu.VMEM((length, 2 * HEAD), jnp.float32),
            pltpu.VMEM((length, 2 * HEAD), jnp.float32),
        ],
        compiler_params=pltpu.CompilerParams(vmem_limit_bytes=VMEM_BYTES),
        cost_estimate=estimate(22),
        name="attend_backward",
    )(slopes, qkv, qkv, qkv, grad, wide, log, *deps)

GELU_RATE = math.sqrt(2.0 / math.pi)
GELU_CUBE = 0.044715
CONTRACT_LAST = (((1,), (1,)), ((), ()))


def feed_forward_kernel(groups, table_ref, x_ref, g_ref, bias_ref, *refs):
    outs, scratch = refs[-11:-4], refs[-4:]
    chips = table_ref.shape[0] // 2
    down_refs, up_refs = refs[: 2 * groups], refs[2 * groups : -11]
    up_groups = len(up_refs) // 2
    layer_ref, back_ref, down_keep, down_send, up_keep, up_send, bias_out = outs
    x_turn, up_tile, down_tile, grad_tile = scratch
    step = pl.program_id(0)
    core = table_ref[2 * chips]
    size = chips // groups
    owned = up_refs[0].shape[1]
    span = down_refs[0].shape[1]

    @pl.when(step == 0)
    def _():
        x_turn[...] = x_ref[...].T
        layer_ref[...] = jnp.zeros_like(layer_ref)
        back_ref[...] = jnp.zeros_like(back_ref)

    def up_rows(place, who):
        start = table_ref[chips + place] * (CORES * owned) + who * owned
        return pl.ds(pl.multiple_of(start, owned), owned)

    for place in range(chips):
        group, at = divmod(place, chips // up_groups)
        up_tile[up_rows(place, core), :] = up_refs[group][at]
        up_tile[up_rows(place, 1 - core), :] = up_refs[up_groups + group][at]

    def down_rows(who):
        return pl.ds(pl.multiple_of(who * span, span), span)

    for group in range(groups):

        @pl.when(step // size == group)
        def _():
            down_tile[down_rows(core), :] = down_refs[group][0]
            down_tile[down_rows(1 - core), :] = down_refs[groups + group][0]

    upper = _dot(x_ref[...], up_tile[...]) + bias_ref[...]
    square = upper * upper
    turned = jnp.tanh(GELU_RATE * (upper + GELU_CUBE * upper * square))
    lift = 0.5 * (1.0 + turned)
    slope = lift + 0.5 * upper * (1.0 - turned * turned) * (GELU_RATE * (1.0 + 3.0 * GELU_CUBE * square))
    hidden = (upper * lift).astype(jnp.bfloat16)
    grad_upper = lax.dot_general(
        g_ref[...], down_tile[...], CONTRACT_LAST, preferred_element_type=jnp.float32
    ) * slope
    bias_out[...] = jnp.sum(grad_upper, axis=0, keepdims=True)
    upper_low = grad_upper.astype(jnp.bfloat16)
    layer_ref[...] += _dot(hidden, down_tile[...])
    back_ref[...] += lax.dot_general(
        upper_low, up_tile[...], CONTRACT_LAST, preferred_element_type=jnp.float32
    )
    grad_tile[...] = _dot(hidden.T, g_ref[...]).astype(jnp.bfloat16)
    down_keep[0] = grad_tile[down_rows(core), :]
    down_send[0] = grad_tile[down_rows(1 - core), :]
    up_tile[...] = _dot(x_turn[...], upper_low).astype(jnp.bfloat16)
    for place in range(chips):
        up_keep[place] = up_tile[up_rows(place, core), :]
        up_send[place] = up_tile[up_rows(place, 1 - core), :]


def group_place(group, size):
    return lambda s, *t: (jnp.clip(s - group * size, 0, size - 1), 0, 0)


def feed_forward(table, x, g, bias, down, up):
    tokens, width = x.shape
    groups = len(down) // 2
    size = down[0].shape[0]
    owned, inner = up[0].shape[1:]
    chips = groups * size
    span = inner // (chips * CORES)
    tile = CORES * span
    whole = lambda s, t: (0, 0)
    column = lambda s, t: (0, t[s])
    columns = lambda s, t: (0, 0, t[s])
    down_spec = lambda place: pl.BlockSpec((1, span, width), place)
    up_spec = pl.BlockSpec((up[0].shape[0], owned, tile), columns)
    shape = jax.ShapeDtypeStruct
    return pl.pallas_call(
        functools.partial(feed_forward_kernel, groups),
        grid_spec=pltpu.PrefetchScalarGridSpec(
            num_scalar_prefetch=1,
            grid=(chips,),
            in_specs=[
                pl.BlockSpec((tokens, width), whole),
                pl.BlockSpec((tokens, width), whole),
                pl.BlockSpec((1, tile), column),
            ]
            + [down_spec(group_place(group, size)) for group in range(groups)] * 2
            + [up_spec] * len(up),
            out_specs=[
                pl.BlockSpec((tokens, width), whole),
                pl.BlockSpec((tokens, width), whole),
                down_spec(lambda s, t: (s, 0, 0)),
                down_spec(lambda s, t: (s, 0, 0)),
                pl.BlockSpec((chips, owned, tile), columns),
                pl.BlockSpec((chips, owned, tile), columns),
                pl.BlockSpec((1, tile), column),
            ],
            scratch_shapes=[
                pltpu.VMEM((width, tokens), jnp.bfloat16),
                pltpu.VMEM((width, tile), jnp.bfloat16),
                pltpu.VMEM((tile, width), jnp.bfloat16),
                pltpu.VMEM((tile, width), jnp.bfloat16),
            ],
        ),
        out_shape=[
            shape((tokens, width), jnp.float32),
            shape((tokens, width), jnp.float32),
            shape((chips, span, width), jnp.bfloat16),
            shape((chips, span, width), jnp.bfloat16),
            shape((chips, owned, inner), jnp.bfloat16),
            shape((chips, owned, inner), jnp.bfloat16),
            shape((1, inner), jnp.float32),
        ],
        compiler_params=pltpu.CompilerParams(vmem_limit_bytes=VMEM_BYTES),
        cost_estimate=estimate(45),
        name="feed_forward",
    )(table, x, g, bias, *down, *up)


def bits_of(size):
    return [1 << b for b in range(size.bit_length() - 1)]


def swap(value, step):
    axis, bit = step
    return lax.ppermute(value, axis, [(i, i ^ bit) for i in range(lax.axis_size(axis))])


def other_core(value):
    return swap(value, ("core", 1))


def offsets_of(steps, rings):
    found = [0]
    for axis, bit in steps:
        found = found + [o ^ (bit * rings if axis == "seq" else bit) for o in found]
    return found


def grow(value, steps):
    for step in steps:
        value = jnp.concatenate((value, swap(value, step)), axis=0)
    return value


def after(values, *others):
    values = tuple(values)
    return pl.pallas_call(
        lambda *refs: None,
        in_specs=[pl.BlockSpec(memory_space=pl.ANY)] * (len(values) + len(others)),
        out_specs=[pl.BlockSpec(memory_space=pl.ANY)] * len(values),
        out_shape=[jax.ShapeDtypeStruct(value.shape, value.dtype) for value in values],
        input_output_aliases={i: i for i in range(len(values))},
        name="after",
    )(*values, *others)


def direct(value, axis):
    return [value] + [swap(value, (axis, m)) for m in range(1, lax.axis_size(axis))]


def add_low(left, right):
    return (left.astype(jnp.float32) + right.astype(jnp.float32)).astype(jnp.bfloat16)


def collect(groups, axis):
    total = groups[0].astype(jnp.float32)
    for m in range(1, len(groups)):
        total = total + swap(groups[m], (axis, m)).astype(jnp.float32)
    return total


def collect_next(total, axis):
    low = total.astype(jnp.bfloat16)
    own = total[0]
    for m in range(1, total.shape[0]):
        own = own + swap(low[m], (axis, m)).astype(jnp.float32)
    return own


def spread(blocks, axis):
    me = lax.axis_index(axis)
    out = jnp.zeros_like(blocks)
    for m in range(lax.axis_size(axis)):
        block = lax.dynamic_slice_in_dim(blocks, me ^ m, 1, 0)
        came = block if m == 0 else swap(block, (axis, m))
        out = lax.dynamic_update_slice_in_dim(out, came, me ^ m, 0)
    return out


def group_columns(weight, ways):
    rows = weight.shape[0]
    parts = weight.reshape(rows, 3, ways, -1, 2 * HEAD)
    return jnp.transpose(parts, (2, 0, 3, 1, 4)).reshape(ways, rows, -1)


def ungroup_columns(grouped):
    ways, rows, _ = grouped.shape
    parts = grouped.reshape(ways, rows, -1, 3, 2 * HEAD)
    return jnp.transpose(parts, (1, 3, 0, 2, 4)).reshape(rows, -1)


def pair_columns(bias, seq_index, ways):
    parts = bias.reshape(2, ways, -1, 2 * HEAD)
    mine = lax.dynamic_index_in_dim(parts, seq_index, 1, keepdims=False)
    return jnp.stack((mine[0], jnp.zeros_like(mine[0]), mine[1]), axis=1).reshape(-1)


def unpair_columns(sums, seq_index, ways):
    parts = sums.reshape(-1, 3, 2 * HEAD)
    mine = jnp.stack((parts[:, 0], parts[:, 2]))
    out = jnp.zeros((2, ways) + mine.shape[1:], jnp.float32)
    return lax.dynamic_update_slice_in_dim(out, mine[:, None], seq_index, 1).reshape(-1)


def norm_parts(values):
    centre = values - jnp.mean(values, axis=-1, keepdims=True)
    factor = lax.rsqrt(jnp.mean(centre * centre, axis=-1, keepdims=True) + EPSILON)
    return centre * factor, factor


def norm_back(grad, gain, unit, factor):
    turned = grad * gain
    inner = jnp.mean(turned * unit, axis=-1, keepdims=True)
    return factor * (turned - jnp.mean(turned, axis=-1, keepdims=True) - unit * inner)


def project_kernel(ways, table_ref, *refs):
    rows, w_ref, gain_ref, shift_ref, bias_ref = refs[:5]
    qkv_ref, normed_ref, unit_ref, weight_ref = refs[-4:]
    step = pl.program_id(0)
    copies = w_ref.shape[0]
    owned = weight_ref.shape[0] // (ways * copies)

    @pl.when(step == 0)
    def _():
        for place in range(copies):
            for sender in range(ways):
                start = (sender * copies + (table_ref[1] ^ place)) * owned
                weight_ref[pl.ds(pl.multiple_of(start, owned), owned), :] = w_ref[place, sender, :owned, :]

    unit, _ = norm_parts(rows[...].astype(jnp.float32))
    normed = (unit * gain_ref[...] + shift_ref[...]).astype(jnp.bfloat16)
    unit_ref[...] = unit.astype(jnp.bfloat16)
    normed_ref[...] = normed
    qkv_ref[...] = (_dot(normed, weight_ref[...]) + bias_ref[...]).astype(jnp.bfloat16)


def project(table, tokens, packed, gain, shift, bias, ways, owned, deps=()):
    width = tokens.shape[1]
    local = tokens.shape[0] // ways
    copies, _, _, triple = packed.shape
    whole = lambda s, t: (0, 0)
    place = lambda s, t: (s, 0)
    full = lambda array: pl.BlockSpec(array.shape, lambda s, t: (0,) * array.ndim)
    operands = (packed, gain, shift, bias)
    shape = jax.ShapeDtypeStruct
    length = ways * local
    return pl.pallas_call(
        functools.partial(project_kernel, ways),
        grid_spec=pltpu.PrefetchScalarGridSpec(
            num_scalar_prefetch=1,
            grid=(ways,),
            in_specs=[pl.BlockSpec((local, width), place)]
            + [full(array) for array in operands]
            + [pl.BlockSpec(memory_space=pl.ANY)] * len(deps),
            out_specs=[
                pl.BlockSpec((local, triple), place),
                pl.BlockSpec((local, width), place),
                pl.BlockSpec((local, width), place),
                pl.BlockSpec((width, triple), whole),
            ],
        ),
        out_shape=[
            shape((length, triple), jnp.bfloat16),
            shape((length, width), jnp.bfloat16),
            shape((length, width), jnp.bfloat16),
            shape((width, triple), jnp.bfloat16),
        ],
        compiler_params=pltpu.CompilerParams(vmem_limit_bytes=VMEM_BYTES),
        cost_estimate=estimate(9),
        name="project",
    )(table, tokens, *operands, *deps)


def input_grad_kernel(low_ref, high_ref, w_ref, normed_ref, unit_ref, *refs):
    part_ref, weight_ref, sum_ref, bias_ref, total = refs[-5:]
    step = pl.program_id(0)

    @pl.when(step == 0)
    def _():
        total[...] = jnp.zeros_like(total)
        sum_ref[...] = jnp.zeros_like(sum_ref)
        bias_ref[...] = jnp.zeros_like(bias_ref)

    grad = jnp.concatenate((low_ref[...], high_ref[...]), axis=1)
    part = lax.dot_general(grad, w_ref[...], CONTRACT_LAST, preferred_element_type=jnp.float32)
    part_ref[...] = part.astype(jnp.bfloat16)
    total[...] += _dot(normed_ref[...].T, grad)
    sum_ref[0:1] += jnp.sum(part * unit_ref[...].astype(jnp.float32), axis=0, keepdims=True)
    sum_ref[1:2] += jnp.sum(part, axis=0, keepdims=True)
    bias_ref[0:1] += jnp.sum(grad.astype(jnp.float32), axis=0, keepdims=True)

    @pl.when(step == pl.num_programs(0) - 1)
    def _():
        weight_ref[...] = total[...].astype(jnp.bfloat16)


def input_grad(low, high, weight, normed, unit, deps=()):
    length, width = normed.shape
    triple = weight.shape[1]
    rows = 512
    block = lambda columns: pl.BlockSpec((rows, columns), lambda s: (s, 0))
    whole = lambda *size: pl.BlockSpec(size, lambda s: (0, 0))
    shape = jax.ShapeDtypeStruct
    return pl.pallas_call(
        input_grad_kernel,
        grid=(length // rows,),
        in_specs=[block(triple // 2), block(triple // 2), whole(width, triple), block(width), block(width)]
        + [pl.BlockSpec(memory_space=pl.ANY)] * len(deps),
        out_specs=[block(width), whole(width, triple), whole(8, width), whole(8, triple)],
        out_shape=[
            shape((length, width), jnp.bfloat16),
            shape((width, triple), jnp.bfloat16),
            shape((8, width), jnp.float32),
            shape((8, triple), jnp.float32),
        ],
        scratch_shapes=[pltpu.VMEM((width, triple), jnp.float32)],
        compiler_params=pltpu.CompilerParams(vmem_limit_bytes=VMEM_BYTES),
        cost_estimate=estimate(10),
        name="input_grad",
    )(low, high, weight, normed, unit, *deps)


def output_rows(table_ref, place, who, owned):
    start = table_ref[place] * (CORES * owned) + who * owned
    return pl.ds(pl.multiple_of(start, owned), owned)


def join_groups(ref):
    return jnp.concatenate([ref[s] for s in range(ref.shape[0])], axis=1)


def output_kernel(table_ref, context_ref, x_ref, bias_ref, gain_ref, shift_ref, *refs):
    residual_ref, normed_ref, weight_ref = refs[-3:]
    parts = refs[:-3]
    groups = len(parts) // 2
    size, owned, _ = parts[0].shape
    core = table_ref[2 * groups * size]

    @pl.when(pl.program_id(0) == 0)
    def _():
        for place in range(groups * size):
            group, at = divmod(place, size)
            weight_ref[output_rows(table_ref, place, core, owned), :] = parts[group][at]
            weight_ref[output_rows(table_ref, place, 1 - core, owned), :] = parts[groups + group][at]

    branch = _dot(join_groups(context_ref), weight_ref[...]) + bias_ref[...]
    residual = x_ref[...].astype(jnp.float32) + branch
    residual_ref[...] = residual
    unit, _ = norm_parts(residual)
    normed_ref[...] = (unit * gain_ref[...] + shift_ref[...]).astype(jnp.bfloat16)


def project_output(table, context, parts, first, x, bias, gain, shift):
    local, width = x.shape
    ways = context.shape[0]
    rows = 256
    vector = pl.BlockSpec((1, width), lambda s, t: (0, 0))
    block = pl.BlockSpec((rows, width), lambda s, t: (s, 0))
    heads = pl.BlockSpec((ways, rows, width // ways), lambda s, t: (0, s, 0))
    size, total, _ = parts[0].shape
    owned = total - first
    weight = pl.BlockSpec((size, owned, width), lambda s, t: (0, first // owned, 0))
    shape = jax.ShapeDtypeStruct
    return pl.pallas_call(
        output_kernel,
        grid_spec=pltpu.PrefetchScalarGridSpec(
            num_scalar_prefetch=1,
            grid=(local // rows,),
            in_specs=[heads, block, vector, vector, vector] + [weight] * len(parts),
            out_specs=[block, block, pl.BlockSpec((width, width), lambda s, t: (0, 0))],
        ),
        out_shape=[
            shape((local, width), jnp.float32),
            shape((local, width), jnp.bfloat16),
            shape((width, width), jnp.bfloat16),
        ],
        compiler_params=pltpu.CompilerParams(vmem_limit_bytes=VMEM_BYTES),
        cost_estimate=estimate(5),
        name="project_output",
    )(table, context, x, bias, gain, shift, *parts)


def residual_kernel(table_ref, grad_ref, residual_ref, up_ref, context_ref, w_ref, gain_ref, *refs):
    out_ref, context_grad_ref, keep_ref, send_ref, sum_ref, total, held = refs[-7:]
    step = pl.program_id(0)
    chips, owned, _ = keep_ref.shape
    ways = context_ref.shape[0]
    core = table_ref[2 * chips]

    @pl.when(step == 0)
    def _():
        total[...] = jnp.zeros_like(total)
        sum_ref[...] = jnp.zeros_like(sum_ref)

    unit, factor = norm_parts(residual_ref[...])
    grad = grad_ref[...]
    upstream = up_ref[...].astype(jnp.float32)
    through = upstream + norm_back(grad, gain_ref[...], unit, factor)
    out_ref[...] = through
    branch = through.astype(jnp.bfloat16)
    context_grad = lax.dot_general(
        branch, w_ref[...], CONTRACT_LAST, preferred_element_type=jnp.float32
    ).astype(jnp.bfloat16)
    wide = context_grad.shape[1] // ways
    for s in range(ways):
        context_grad_ref[s] = context_grad[:, s * wide : (s + 1) * wide]
    total[...] += _dot(join_groups(context_ref).T, branch)
    for row, term in enumerate((grad * unit, grad, through, upstream)):
        sum_ref[row : row + 1] += jnp.sum(term, axis=0, keepdims=True)

    @pl.when(step == pl.num_programs(0) - 1)
    def _():
        held[...] = total[...].astype(jnp.bfloat16)
        for place in range(chips):
            keep_ref[place] = held[output_rows(table_ref, place, core, owned), :]
            send_ref[place] = held[output_rows(table_ref, place, 1 - core, owned), :]


def residual_grad(table, grad, residual, upstream, context, weight, gain, chips):
    local, width = residual.shape
    ways = context.shape[0]
    rows = 256
    owned = width // (chips * CORES)
    whole = lambda *size: pl.BlockSpec(size, lambda s, t: (0,) * len(size))
    block = pl.BlockSpec((rows, width), lambda s, t: (s, 0))
    heads = pl.BlockSpec((ways, rows, width // ways), lambda s, t: (0, s, 0))
    shape = jax.ShapeDtypeStruct
    return pl.pallas_call(
        residual_kernel,
        grid_spec=pltpu.PrefetchScalarGridSpec(
            num_scalar_prefetch=1,
            grid=(local // rows,),
            in_specs=[block, block, block, heads, whole(width, width), whole(1, width)],
            out_specs=[block, heads, whole(chips, owned, width), whole(chips, owned, width), whole(8, width)],
            scratch_shapes=[pltpu.VMEM((width, width), jnp.float32), pltpu.VMEM((width, width), jnp.bfloat16)],
        ),
        out_shape=[
            shape((local, width), jnp.float32),
            shape((ways, local, width // ways), jnp.bfloat16),
            shape((chips, owned, width), jnp.bfloat16),
            shape((chips, owned, width), jnp.bfloat16),
            shape((8, width), jnp.float32),
        ],
        compiler_params=pltpu.CompilerParams(vmem_limit_bytes=VMEM_BYTES),
        cost_estimate=estimate(7),
        name="residual_grad",
    )(table, grad, residual, upstream, context, weight, gain)


def meet_kernel(groups, up_groups, down_keep, down_came, output_keep, output_came, up_keep, up_came, *refs):
    step = pl.program_id(0)
    size = pl.num_programs(0) // groups
    span = down_keep.shape[1]

    def both(left, right):
        return (left[0].astype(jnp.float32) + right[0].astype(jnp.float32)).astype(jnp.bfloat16)

    for group in range(groups):

        @pl.when(step // size == group)
        def _():
            refs[group][0, :span] = both(down_keep, down_came)
            refs[group][0, span:] = both(output_keep, output_came)

    for group in range(up_groups):

        @pl.when(step // (pl.num_programs(0) // up_groups) == group)
        def _():
            refs[groups + group][0] = both(up_keep, up_came)


def meet(down_keep, down_came, output_keep, output_came, up_keep, up_came, groups, up_groups):
    chips, span, width = down_keep.shape
    owned, inner = up_keep.shape[1:]
    block = lambda rows, columns: pl.BlockSpec((1, rows, columns), lambda s: (s, 0, 0))
    parts = [(span + owned, width, chips // groups, group) for group in range(groups)]
    parts += [(owned, inner, chips // up_groups, group) for group in range(up_groups)]
    outs = [pl.BlockSpec((1, rows, columns), group_place(group, size)) for rows, columns, size, group in parts]
    shapes = [jax.ShapeDtypeStruct((size, rows, columns), jnp.bfloat16) for rows, columns, size, _ in parts]
    return pl.pallas_call(
        functools.partial(meet_kernel, groups, up_groups),
        grid=(chips,),
        in_specs=[block(span, width)] * 2 + [block(owned, width)] * 2 + [block(owned, inner)] * 2,
        out_specs=outs,
        out_shape=shapes,
        compiler_params=pltpu.CompilerParams(vmem_limit_bytes=VMEM_BYTES),
        cost_estimate=estimate(9),
        name="meet",
    )(down_keep, down_came, output_keep, output_came, up_keep, up_came)


def halve(value, step, kind):
    axis, bit = step
    mine = (lax.axis_index(axis) // bit) % 2
    sent = lax.dynamic_index_in_dim(value, 1 - mine, 0, keepdims=False).astype(kind)
    kept = lax.dynamic_index_in_dim(value, mine, 0, keepdims=False)
    return kept.astype(jnp.float32) + swap(sent, step).astype(jnp.float32)


def scatter_copies(value, kind):
    rings = lax.axis_size("ring")
    value = jnp.moveaxis(value.reshape((rings, CORES) + value.shape[1:]), 1, 0)
    value = halve(value, ("core", 1), kind)
    for bit in bits_of(rings):
        shape = value.shape
        value = jnp.moveaxis(value.reshape((shape[0] // 2, 2) + shape[1:]), 1, 0)
        value = halve(value, ("ring", bit), kind)
    return value[0]


def scatter_seq(value, kind):
    for bit in reversed(bits_of(lax.axis_size("seq"))):
        value = halve(value.reshape((2, value.shape[0] // 2) + value.shape[1:]), ("seq", bit), kind)
    return value[0]


def layer_norm(values, norm_gain, norm_shift):
    centre = values - jnp.mean(values, axis=-1, keepdims=True)
    spread = jnp.mean(centre * centre, axis=-1, keepdims=True)
    return centre * lax.rsqrt(spread + EPSILON) * norm_gain + norm_shift


def tanh_gelu(upper_in):
    return jax.nn.gelu(upper_in, approximate=True)


def gather_small(parts):
    sizes = [part.shape[0] for part in parts]
    width = -(-sum(sizes) // 512) * 512
    packed = jnp.concatenate(list(parts) + [jnp.zeros((width - sum(sizes),), parts[0].dtype)])
    whole = lax.all_gather(packed.reshape(4, width // 4), WORLD, axis=0, tiled=False)
    whole = whole.reshape(-1, width).astype(jnp.float32)
    out, start = [], 0
    for size in sizes:
        out.append(whole[:, start : start + size].reshape(-1))
        start += size
    return out


def scatter_small(parts, world):
    rows = [part.reshape(world, -1) for part in parts]
    sizes = [row.shape[1] for row in rows]
    width = -(-sum(sizes) // 128) * 128
    packed = jnp.concatenate(rows + [jnp.zeros((world, width - sum(sizes)), jnp.float32)], axis=1)
    owned = lax.psum_scatter(packed, WORLD, scatter_dimension=0, tiled=True)[0]
    out, start = [], 0
    for size in sizes:
        out.append(owned[start : start + size])
        start += size
    return out


def gather_weight(shard):
    mine = lax.all_gather(shard, CHIPS, axis=0, tiled=False)
    theirs = other_core(mine)
    first = lax.axis_index("core") == 0
    pair = jnp.stack((jnp.where(first, mine, theirs), jnp.where(first, theirs, mine)), axis=1)
    return pair.reshape(-1, shard.shape[-1])


def pick_rows(columns, chips, core):
    tokens, width = columns.shape
    parts = columns.reshape(tokens, chips, CORES, width // (chips * CORES))
    return lax.dynamic_index_in_dim(parts, core, 2, keepdims=False).reshape(tokens, width // CORES)


def contract_tokens(left, right):
    return lax.dot_general(left, right, (((0,), (0,)), ((), ())), preferred_element_type=jnp.float32)


def scatter_weight_grad(left, right, chips):
    core = lax.axis_index("core")
    sent = contract_tokens(pick_rows(left, chips, 1 - core), right).astype(jnp.bfloat16)
    came = other_core(sent).astype(jnp.float32)
    both = (contract_tokens(pick_rows(left, chips, core), right) + came).astype(jnp.bfloat16)
    return lax.psum_scatter(both, CHIPS, scatter_dimension=0, tiled=True).astype(jnp.float32)


def plain_body(
    tokens_in,
    out_grad,
    first_gain,
    first_shift,
    input_weight,
    input_bias,
    output_weight,
    output_bias,
    second_gain,
    second_shift,
    up_weight,
    up_bias,
    down_weight,
    down_bias,
):
    ways = lax.axis_size("seq")
    rings = lax.axis_size("ring")
    chips = ways * rings
    model_width = tokens_in.shape[-1]
    group_width = model_width // ways
    head_group = group_width // HEAD
    rows_in = tokens_in.reshape(-1, model_width)
    local = rows_in.shape[0]
    length = local * ways
    upstream = out_grad.reshape(local, model_width)

    (
        gain_first,
        shift_first,
        bias_input,
        bias_output,
        gain_second,
        shift_second,
        bias_up,
        bias_down,
    ) = gather_small(
        (first_gain, first_shift, input_bias, output_bias, second_gain, second_shift, up_bias, down_bias)
    )
    seq_index = lax.axis_index("seq")

    all_rows = lax.all_gather(rows_in, "seq", axis=0, tiled=True)
    owned_rows = input_weight.shape[0]
    by_group = group_columns(input_weight, ways)
    columns = lax.all_to_all(by_group, "seq", split_axis=0, concat_axis=0, tiled=True)
    columns = lax.all_gather(columns, ("ring", "core"), axis=0, tiled=False)
    weight_input = jnp.moveaxis(columns, 0, 1).reshape(model_width, 3 * group_width)

    weight_output = gather_weight(output_weight)
    weight_up = gather_weight(up_weight)
    weight_down = gather_weight(down_weight)

    normed = layer_norm(all_rows.astype(jnp.float32), gain_first, shift_first).astype(jnp.bfloat16)
    bias_group = pair_columns(bias_input, seq_index, ways)
    qkv = (jnp.dot(normed, weight_input, preferred_element_type=jnp.float32) + bias_group).astype(
        jnp.bfloat16
    )
    head_ids = (seq_index * head_group + jnp.arange(head_group, dtype=jnp.int32)).astype(jnp.float32)
    slopes = jnp.exp2(-8.0 * (head_ids + 1.0) / HEADS)
    pairs = range(head_group // 2)
    kept = [attend_forward(slopes[2 * p : 2 * p + 2], qkv, p) for p in pairs]
    context_split = jnp.concatenate([k[0] for k in kept], axis=1)
    context = lax.all_to_all(
        context_split.reshape(ways, local, group_width), "seq", split_axis=0, concat_axis=0, tiled=True
    )
    context = jnp.moveaxis(context, 0, 1).reshape(local, model_width)

    inputs = rows_in.astype(jnp.float32)
    branch = jnp.dot(context, weight_output, preferred_element_type=jnp.float32) + bias_output
    residual = inputs + branch
    normed_two_float, second_back = jax.vjp(layer_norm, residual, gain_second, shift_second)
    normed_two = normed_two_float.astype(jnp.bfloat16)
    upper = jnp.dot(normed_two, weight_up, preferred_element_type=jnp.float32) + bias_up
    activated, gelu_back = jax.vjp(tanh_gelu, upper)
    hidden = activated.astype(jnp.bfloat16)
    layer_out = (
        residual + jnp.dot(hidden, weight_down, preferred_element_type=jnp.float32) + bias_down
    ).astype(jnp.bfloat16)
    grad_hidden = lax.dot_general(
        upstream, weight_down, (((1,), (1,)), ((), ())), preferred_element_type=jnp.float32
    )
    grad_upper = gelu_back(grad_hidden)[0]
    upper_low = grad_upper.astype(jnp.bfloat16)
    grad_normed_two = lax.dot_general(
        upper_low, weight_up, (((1,), (1,)), ((), ())), preferred_element_type=jnp.float32
    )
    grad_through, grad_second_gain, grad_second_shift = second_back(grad_normed_two)
    grad_residual = upstream.astype(jnp.float32) + grad_through
    branch_low = grad_residual.astype(jnp.bfloat16)
    context_grad = lax.dot_general(
        branch_low, weight_output, (((1,), (1,)), ((), ())), preferred_element_type=jnp.float32
    ).astype(jnp.bfloat16)
    grad_split = jnp.moveaxis(context_grad.reshape(local, ways, group_width), 1, 0)
    grad_split = lax.all_to_all(grad_split, "seq", split_axis=0, concat_axis=0, tiled=True)
    grad_split = grad_split.reshape(length, group_width)

    grad_down_weight = scatter_weight_grad(hidden, upstream, chips)
    grad_up_weight = scatter_weight_grad(normed_two, upper_low, chips)
    grad_output_weight = scatter_weight_grad(context, branch_low, chips)

    grad_qkv = jnp.concatenate(
        [
            attend_backward(
                slopes[2 * p : 2 * p + 2], qkv, grad_split, kept[p][1], kept[p][2], p
            )
            for p in pairs
        ],
        axis=1,
    )

    grad_normed = lax.dot_general(
        grad_qkv, weight_input, (((1,), (1,)), ((), ())), preferred_element_type=jnp.float32
    ).astype(jnp.bfloat16)
    grad_normed = lax.all_to_all(
        grad_normed.reshape(ways, local, model_width), "seq", split_axis=0, concat_axis=0, tiled=True
    )
    grad_normed = jnp.sum(grad_normed.astype(jnp.float32), axis=0)

    grad_columns = contract_tokens(normed, grad_qkv)
    grad_columns = jnp.moveaxis(
        grad_columns.reshape(ways, rings * CORES, owned_rows, 3 * group_width), 1, 0
    ).astype(jnp.bfloat16)
    grad_columns = lax.psum_scatter(
        grad_columns.reshape(-1, 3 * group_width), ("ring", "core"), scatter_dimension=0, tiled=True
    )
    grad_columns = lax.all_to_all(
        grad_columns.reshape(ways, owned_rows, 3 * group_width), "seq", split_axis=0, concat_axis=0, tiled=True
    )
    grad_input_weight = ungroup_columns(grad_columns).astype(jnp.float32)
    grad_input_bias = unpair_columns(jnp.sum(grad_qkv.astype(jnp.float32), axis=0), seq_index, ways)
    _, first_back = jax.vjp(layer_norm, inputs, gain_first, shift_first)
    grad_entry, grad_first_gain, grad_first_shift = first_back(grad_normed)
    tokens_grad = grad_residual + grad_entry

    small = scatter_small(
        (
            grad_first_gain,
            grad_first_shift,
            grad_input_bias,
            jnp.sum(grad_residual, axis=0),
            grad_second_gain,
            grad_second_shift,
            jnp.sum(grad_upper, axis=0),
            jnp.sum(upstream.astype(jnp.float32), axis=0),
        ),
        chips * CORES,
    )
    return (
        layer_out.reshape(tokens_in.shape),
        tokens_grad.reshape(tokens_in.shape),
        small[0],
        small[1],
        grad_input_weight,
        small[2],
        grad_output_weight,
        small[3],
        small[4],
        small[5],
        grad_up_weight,
        small[6],
        grad_down_weight,
        small[7],
    )


def blocked_body(
    tokens_in,
    out_grad,
    first_gain,
    first_shift,
    input_weight,
    input_bias,
    output_weight,
    output_bias,
    second_gain,
    second_shift,
    up_weight,
    up_bias,
    down_weight,
    down_bias,
):
    ways = lax.axis_size("seq")
    rings = lax.axis_size("ring")
    chips = ways * rings
    copies = rings * CORES
    world = chips * CORES
    model_width = tokens_in.shape[-1]
    head_group = model_width // ways // HEAD
    rows_in = tokens_in.reshape(-1, model_width)
    local = rows_in.shape[0]
    length = local * ways
    upstream = out_grad.reshape(local, model_width)
    seq_index = lax.axis_index("seq")
    core = lax.axis_index("core")
    chip_index = seq_index * rings + lax.axis_index("ring")
    copy_index = lax.axis_index("ring") * CORES + core

    ring = lax.axis_index("ring")
    far_bit, near_bit = rings // 2, 1
    down_away = [s * rings + r for s in range(ways) for r in range(rings)]
    up_away = [s * rings + near + far for near in (0, near_bit) for s in range(ways) for far in (0, far_bit)]
    down_table, up_table = (jnp.array(away, jnp.int32) ^ chip_index for away in (down_away, up_away))
    table = jnp.concatenate((down_table, up_table, core[None]))

    vectors = (first_gain, first_shift, input_bias, output_bias, second_gain, second_shift, up_bias, down_bias)
    sizes = [vector.shape[0] for vector in vectors]
    owned = input_weight.shape[0]
    by_group = group_columns(input_weight, ways)
    triple = by_group.shape[-1]
    packed = jnp.concatenate([jnp.pad(vector, (0, 128 - vector.shape[0]))[None] for vector in vectors])
    packed = jnp.pad(packed, ((0, 8 - len(sizes)), (0, triple - 128)))
    by_group = jnp.concatenate((by_group, jnp.broadcast_to(packed[None], (ways, 8, triple))), axis=1)
    owned_down = down_weight.shape[0]
    down_shard = jnp.concatenate((down_weight, output_weight))
    grouped = spread(by_group, "seq")
    columns = grouped[None]
    for bit in (far_bit, near_bit):
        columns = jnp.stack((columns, swap(columns, ("ring", bit))), axis=1).reshape((-1,) + by_group.shape)
    up_one = jnp.stack((up_weight, swap(up_weight, ("ring", far_bit))))
    down_one = jnp.stack(direct(down_shard, "ring"))
    columns = jnp.stack((columns, other_core(columns)), axis=1).reshape((copies,) + by_group.shape)
    found = columns[:, :, owned : owned + len(sizes), :128].reshape(world, -1)
    here = jnp.arange(world, dtype=jnp.int32)
    wanted = ((here % copies) ^ copy_index) * ways + here // copies
    pick = (wanted[:, None] == here[None, :]).astype(jnp.bfloat16)
    found = jnp.dot(pick, found, preferred_element_type=jnp.float32)
    vectors = [found[:, 128 * i : 128 * i + size].reshape(1, -1) for i, size in enumerate(sizes)]
    gain_first, shift_first, bias_input, bias_output, gain_second, shift_second, bias_up, bias_down = vectors
    bias_group = pair_columns(bias_input[0], seq_index, ways)[None]

    all_rows = lax.all_gather(rows_in, "seq", tiled=True)

    up_near = jnp.concatenate(direct(up_one, "seq"))
    (down_one,) = after((down_one,), all_rows)
    (up_near,) = after((up_near,), columns)
    down_mine = direct(down_one, "seq")
    up_far = swap(up_near, ("ring", near_bit))

    places = jnp.stack((seq_index, copy_index)).astype(jnp.int32)
    qkv, normed, unit, weight_input = project(
        places, all_rows, columns, gain_first, shift_first, bias_group, ways, owned, (down_one, up_near)
    )
    head_ids = (seq_index * head_group + jnp.arange(head_group, dtype=jnp.int32)).astype(jnp.float32)
    slopes = jnp.exp2(-8.0 * (head_ids + 1.0) / HEADS)

    def exchange(value):
        return lax.all_to_all(
            value.reshape(ways, local, -1), "seq", split_axis=0, concat_axis=0, tiled=True
        )

    kept, contexts, done = [], [], ()
    for pair in range(2):
        context, wide, log_totals = attend_forward(slopes[2 * pair : 2 * pair + 2], qkv, pair, done)
        kept.append((wide, log_totals))
        contexts.append(context)
        done = (log_totals,)
    context = exchange(jnp.concatenate(contexts, axis=1))

    mine = list(after(down_mine + [up_near, up_far], context))
    theirs = [other_core(group) for group in mine]
    down = mine[:ways] + theirs[:ways]
    up = mine[ways:] + theirs[ways:]
    residual, normed_two, weight_output = project_output(
        table, context, down, owned_down, rows_in, bias_output, gain_second, shift_second
    )
    layer, grad_normed_two, down_keep, down_send, up_keep, up_send, grad_up_bias = feed_forward(
        table, normed_two, upstream, bias_up, down, up
    )
    grad_residual, context_grad, output_keep, output_send, middle_sums = residual_grad(
        table, grad_normed_two, residual, upstream, context, weight_output, gain_second, chips
    )
    layer_out = (residual + layer + bias_down).astype(jnp.bfloat16)

    context_grad = exchange(context_grad).reshape(length, -1)
    met = list(
        meet(down_keep, other_core(down_send), output_keep, other_core(output_send), up_keep, other_core(up_send), ways, 2)
    )
    met = list(after(met, context_grad))
    came = [swap(met[m], ("seq", m)) for m in range(1, ways)] + [swap(met[ways + 1], ("ring", near_bit))]

    grads = []
    for pair in range(2):
        ready = grads + [met[0]]
        grads.append(attend_backward(slopes[2 * pair : 2 * pair + 2], qkv, context_grad, *kept[pair], pair, ready))
    came = after(came, grads[1])
    down_sum = met[0].astype(jnp.float32)
    for part in came[: ways - 1]:
        down_sum = down_sum + part.astype(jnp.float32)
    down_sum = down_sum.astype(jnp.bfloat16)
    up_sum = (met[ways].astype(jnp.float32) + came[ways - 1].astype(jnp.float32)).astype(jnp.bfloat16)
    up_sum = up_sum.reshape((ways, 2) + up_sum.shape[1:])

    part, grad_columns, first_sums, bias_sums = input_grad(
        grads[0], grads[1], weight_input, normed, unit, (down_sum, up_sum)
    )
    down_sum = collect_next(down_sum, "ring")
    up_sum = collect_next(up_sum, "seq")
    grad_up_weight = up_sum[0] + swap(up_sum[1].astype(jnp.bfloat16), ("ring", far_bit)).astype(jnp.float32)
    grad_down_weight, grad_output_weight = down_sum[:owned_down], down_sum[owned_down:]
    grad_normed = jnp.sum(exchange(part).astype(jnp.float32), axis=0)
    inputs = rows_in.astype(jnp.float32)
    tokens_grad = grad_residual + norm_back(grad_normed, gain_first, *norm_parts(inputs))

    sums = (
        first_sums[0],
        first_sums[1],
        unpair_columns(bias_sums[0], seq_index, ways),
        middle_sums[2],
        middle_sums[0],
        middle_sums[1],
        grad_up_bias[0],
        middle_sums[3],
    )
    rows = [jnp.pad(term.reshape(world, -1), ((0, 0), (0, 128 - size))) for term, size in zip(sums, sizes)]
    rows = jnp.stack(rows, axis=1).astype(jnp.bfloat16)
    rows = jnp.pad(rows, ((0, 0), (0, 8 - len(sizes)), (0, triple - 128)))
    both = jnp.concatenate((grad_columns.reshape(world, owned, triple), rows), axis=1)
    both = both.reshape(ways, rings, CORES, owned + 8, triple)
    came = other_core(lax.dynamic_index_in_dim(both, 1 - core, 2, keepdims=False))
    both = add_low(lax.dynamic_index_in_dim(both, core, 2, keepdims=False), came)
    ring = lax.axis_index("ring")
    both = collect([lax.dynamic_index_in_dim(both, ring ^ m, 1, keepdims=False) for m in range(rings)], "ring")
    both = spread(both.astype(jnp.bfloat16), "seq")
    grad_input_weight = ungroup_columns(both[:, :owned]).astype(jnp.float32)
    rows = jnp.sum(both[:, owned:, :128].astype(jnp.float32), axis=0)
    small = [rows[i, :size] for i, size in enumerate(sizes)]
    return (
        layer_out.reshape(tokens_in.shape),
        tokens_grad.reshape(tokens_in.shape),
        small[0],
        small[1],
        grad_input_weight,
        small[2],
        grad_output_weight,
        small[3],
        small[4],
        small[5],
        grad_up_weight,
        small[6],
        grad_down_weight,
        small[7],
    )


def solution(mesh):
    ways, copies = mesh.shape["seq"], mesh.shape["dp"]
    split = Mesh(mesh.devices.reshape(ways, copies // CORES, CORES), WORLD)
    token = P(("ring", "core"), "seq", None)
    vector = P(WORLD)
    matrix = P(WORLD, None)
    weights = (vector, vector, matrix, vector, matrix, vector, vector, vector, matrix, vector, matrix, vector)
    step = blocked_body if ways == 4 else plain_body
    return jax.shard_map(
        step,
        mesh=split,
        in_specs=(token, token) + weights,
        out_specs=(token, token) + weights,
        check_vma=False,
    )
```

```python
import functools
import math

import jax
import jax.numpy as jnp
from jax import lax
from jax.experimental import pallas as pl
from jax.experimental.pallas import tpu as pltpu
from jax.sharding import Mesh
from jax.sharding import PartitionSpec as P

HEADS = 16
HEAD = 64
EPSILON = 1e-05
LOG2E = math.log2(math.e)
TILE = 256
VMEM_BYTES = 60 * 1024 * 1024
CORES = 2
CHIPS = ("seq", "ring")
WORLD = ("seq", "ring", "core")

def _dot(a, b):
    return jnp.dot(a, b, preferred_element_type=jnp.float32)

def _bias_tile(slope):
    return lax.broadcasted_iota(jnp.int32, (TILE, TILE), 0).astype(jnp.float32) * slope

def _keep():
    return lax.broadcasted_iota(jnp.int32, (TILE, TILE), 0) <= lax.broadcasted_iota(jnp.int32, (TILE, TILE), 1)

def _row_mask(shape, axis, half):
    ids = lax.broadcasted_iota(jnp.int32, shape, axis)
    return (ids >= HEAD) == (half == 1)

def estimate(micros):
    return pl.CostEstimate(flops=int(micros * 1e8), bytes_accessed=0, transcendentals=0)

def forward_kernel(slope_ref, q_ref, k_ref, v_ref, *refs):
    ctx_ref, wide_ref, log_ref, q_turn, v_turn, scores = refs[-6:]
    head = pl.program_id(0)
    half = lax.rem(head, 2)
    length = q_ref.shape[0]
    tiles = length // TILE

    @pl.when(half == 0)
    def _():
        q_turn[...] = q_ref[...].T
        v_turn[...] = v_ref[...].T

    slope = slope_ref[head] * LOG2E
    scale = HEAD ** -0.5 * LOG2E
    rows = pl.ds(pl.multiple_of(half * HEAD, HEAD), HEAD)
    bias = _bias_tile(slope)
    for i in range(tiles):
        cols = slice(i * TILE, (i + 1) * TILE)
        q_block = q_turn[:, cols]
        q_block = jnp.where(_row_mask(q_block.shape, 0, half), q_block, jnp.zeros_like(q_block))
        peak = None
        for c in range(i + 1):
            part = _dot(k_ref[c * TILE:(c + 1) * TILE, :], q_block) * scale + bias
            if c == i:
                part = jnp.where(_keep(), part, -jnp.inf)
            scores[i % 2, c] = part
            top = jnp.max(part, axis=0, keepdims=True) + slope * ((c - i) * TILE)
            peak = top if peak is None else jnp.maximum(peak, top)
        total = jnp.zeros((1, TILE), jnp.float32)
        out = jnp.zeros((HEAD, TILE), jnp.float32)
        for c in range(i + 1):
            probs = jnp.exp2(scores[i % 2, c] - (peak - slope * ((c - i) * TILE)))
            total = total + jnp.sum(probs, axis=0, keepdims=True)
            out = out + _dot(v_turn[rows, c * TILE:(c + 1) * TILE], probs.astype(jnp.bfloat16))
        wide_ref[rows, cols] = out / total
        log_ref[:, cols] = jnp.broadcast_to(peak + jnp.log2(total), (8, TILE))

    @pl.when(half == 1)
    def _():
        ctx_ref[...] = wide_ref[...].T.astype(jnp.bfloat16)

def attend_forward(slopes, qkv, pair, deps=()):
    length = qkv.shape[0]
    spec = lambda part: pl.BlockSpec((length, 2 * HEAD), lambda h: (0, 3 * pair + part))
    return pl.pallas_call(
        forward_kernel,
        grid=(2,),
        in_specs=[pl.BlockSpec(memory_space=pltpu.SMEM), spec(0), spec(1), spec(2)]
        + [pl.BlockSpec(memory_space=pl.ANY)] * len(deps),
        out_specs=[
            pl.BlockSpec((length, 2 * HEAD), lambda h: (0, 0)),
            pl.BlockSpec((2 * HEAD, length), lambda h: (0, 0)),
            pl.BlockSpec((8, length), lambda h: (h, 0)),
        ],
        out_shape=[
            jax.ShapeDtypeStruct((length, 2 * HEAD), jnp.bfloat16),
            jax.ShapeDtypeStruct((2 * HEAD, length), jnp.float32),
            jax.ShapeDtypeStruct((2 * 8, length), jnp.float32),
        ],
        scratch_shapes=[
            pltpu.VMEM((2 * HEAD, length), jnp.bfloat16),
            pltpu.VMEM((2 * HEAD, length), jnp.bfloat16),
            pltpu.VMEM((2, length // TILE, TILE, TILE), jnp.float32),
        ],
        compiler_params=pltpu.CompilerParams(vmem_limit_bytes=VMEM_BYTES),
        cost_estimate=estimate(10.5),
        name="attend_forward",
    )(slopes, qkv, qkv, qkv, *deps)

def backward_kernel(slope_ref, q_ref, k_ref, v_ref, g_ref, wide_ref, log_ref, *refs):
    out_ref, q_turn, k_turn, g_turn, dq_turn, dk_sum, dv_sum = refs[-7:]
    head = pl.program_id(0)
    half = lax.rem(head, 2)
    length = q_ref.shape[0]
    tiles = length // TILE
    wide = 2 * HEAD

    @pl.when(half == 0)
    def _():
        q_turn[...] = q_ref[...].T
        k_turn[...] = k_ref[...].T
        g_turn[...] = g_ref[...].T

    slope = slope_ref[head] * LOG2E
    scale = HEAD ** -0.5 * LOG2E
    rows = pl.ds(pl.multiple_of(half * HEAD, HEAD), HEAD)
    bias = _bias_tile(slope)
    inner = jnp.sum(wide_ref[rows, :] * g_turn[rows, :].astype(jnp.float32), axis=0, keepdims=True)
    for c in range(tiles):
        span = slice(c * TILE, (c + 1) * TILE)
        dk = jnp.zeros((TILE, 2 * HEAD), jnp.float32)
        dv = jnp.zeros((TILE, 2 * HEAD), jnp.float32)
        for i in range(c, tiles):
            cols = slice(i * TILE, (i + 1) * TILE)
            q_cols = q_turn[:, cols]
            q_cols = jnp.where(_row_mask(q_cols.shape, 0, half), q_cols, jnp.zeros_like(q_cols))
            g_cols = g_turn[:, cols]
            g_cols = jnp.where(_row_mask(g_cols.shape, 0, half), g_cols, jnp.zeros_like(g_cols))
            q_rows = q_ref[cols, :]
            q_rows = jnp.where(_row_mask(q_rows.shape, 1, half), q_rows, jnp.zeros_like(q_rows))
            g_rows = g_ref[cols, :]
            g_rows = jnp.where(_row_mask(g_rows.shape, 1, half), g_rows, jnp.zeros_like(g_rows))
            part = _dot(k_ref[span, :], q_cols) * scale + bias
            if c == i:
                part = jnp.where(_keep(), part, -jnp.inf)
            probs = jnp.exp2(part - (log_ref[0:1, cols] - slope * ((c - i) * TILE)))
            grad = (probs * (_dot(v_ref[span, :], g_cols) - inner[:, cols])).astype(jnp.bfloat16)
            dv = dv + _dot(probs.astype(jnp.bfloat16), g_rows)
            dk = dk + _dot(grad, q_rows)
            dq = _dot(k_turn[rows, span], grad)
            if c == 0:
                dq_turn[rows, cols] = dq
            else:
                dq_turn[rows, cols] += dq

        @pl.when(half == 0)
        def _():
            dk_sum[span, :] = dk
            dv_sum[span, :] = dv

        @pl.when(half == 1)
        def _():
            out_ref[span, wide : 2 * wide] = ((dk_sum[span, :] + dk) * HEAD ** -0.5).astype(jnp.bfloat16)
            out_ref[span, 2 * wide :] = (dv_sum[span, :] + dv).astype(jnp.bfloat16)

    @pl.when(half == 1)
    def _():
        out_ref[:, :wide] = (dq_turn[...] * HEAD ** -0.5).T.astype(jnp.bfloat16)

def attend_backward(slopes, qkv, grad, wide, log, pair, deps=()):
    length = qkv.shape[0]
    spec = lambda part: pl.BlockSpec((length, 2 * HEAD), lambda h: (0, 3 * pair + part))
    return pl.pallas_call(
        backward_kernel,
        grid=(2,),
        in_specs=[
            pl.BlockSpec(memory_space=pltpu.SMEM), spec(0), spec(1), spec(2),
            pl.BlockSpec((length, 2 * HEAD), lambda h: (0, pair)),
            pl.BlockSpec((2 * HEAD, length), lambda h: (0, 0)),
            pl.BlockSpec((8, length), lambda h: (h, 0)),
        ] + [pl.BlockSpec(memory_space=pl.ANY)] * len(deps),
        out_specs=pl.BlockSpec((length, 6 * HEAD), lambda h: (0, 0)),
        out_shape=jax.ShapeDtypeStruct((length, 6 * HEAD), jnp.bfloat16),
        scratch_shapes=[
            pltpu.VMEM((2 * HEAD, length), jnp.bfloat16),
            pltpu.VMEM((2 * HEAD, length), jnp.bfloat16),
            pltpu.VMEM((2 * HEAD, length), jnp.bfloat16),
            pltpu.VMEM((2 * HEAD, length), jnp.float32),
            pltpu.VMEM((length, 2 * HEAD), jnp.float32),
            pltpu.VMEM((length, 2 * HEAD), jnp.float32),
        ],
        compiler_params=pltpu.CompilerParams(vmem_limit_bytes=VMEM_BYTES),
        cost_estimate=estimate(22),
        name="attend_backward",
    )(slopes, qkv, qkv, qkv, grad, wide, log, *deps)

GELU_RATE = math.sqrt(2.0 / math.pi)
GELU_CUBE = 0.044715
CONTRACT_LAST = (((1,), (1,)), ((), ()))


def feed_forward_kernel(groups, per, table_ref, x_ref, g_ref, bias_ref, *refs):
    outs, scratch = refs[-11:-4], refs[-4:]
    chips = table_ref.shape[0] // 2
    down_refs, up_refs = refs[: 2 * groups], refs[2 * groups : -11]
    up_groups = len(up_refs) // 2
    layer_ref, back_ref, down_keep, down_send, up_keep, up_send, bias_out = outs
    x_turn, up_tile, down_tile, grad_tile = scratch
    step = pl.program_id(0)
    core = table_ref[2 * chips]
    steps = chips // (groups * per)
    owned = up_refs[0].shape[1]
    span = down_refs[0].shape[1]

    @pl.when(step == 0)
    def _():
        x_turn[...] = x_ref[...].T
        layer_ref[...] = jnp.zeros_like(layer_ref)
        back_ref[...] = jnp.zeros_like(back_ref)

    def up_rows(place, who):
        start = table_ref[chips + place] * (CORES * owned) + who * owned
        return pl.ds(pl.multiple_of(start, owned), owned)

    for place in range(chips):
        group, at = divmod(place, chips // up_groups)
        up_tile[up_rows(place, core), :] = up_refs[group][at]
        up_tile[up_rows(place, 1 - core), :] = up_refs[up_groups + group][at]

    def down_rows(at, who):
        chip = lax.rem(table_ref[step * per + at], per)
        return pl.ds(pl.multiple_of((chip * CORES + who) * span, span), span)

    for group in range(groups):

        @pl.when(step // steps == group)
        def _():
            for at in range(per):
                down_tile[down_rows(at, core), :] = down_refs[group][at]
                down_tile[down_rows(at, 1 - core), :] = down_refs[groups + group][at]

    upper = _dot(x_ref[...], up_tile[...]) + bias_ref[...]
    square = upper * upper
    turned = jnp.tanh(GELU_RATE * (upper + GELU_CUBE * upper * square))
    lift = 0.5 * (1.0 + turned)
    slope = lift + 0.5 * upper * (1.0 - turned * turned) * (GELU_RATE * (1.0 + 3.0 * GELU_CUBE * square))
    hidden = (upper * lift).astype(jnp.bfloat16)
    grad_upper = lax.dot_general(
        g_ref[...], down_tile[...], CONTRACT_LAST, preferred_element_type=jnp.float32
    ) * slope
    bias_out[...] = jnp.sum(grad_upper, axis=0, keepdims=True)
    upper_low = grad_upper.astype(jnp.bfloat16)
    layer_ref[...] += _dot(hidden, down_tile[...])
    back_ref[...] += lax.dot_general(
        upper_low, up_tile[...], CONTRACT_LAST, preferred_element_type=jnp.float32
    )
    grad_tile[...] = _dot(hidden.T, g_ref[...]).astype(jnp.bfloat16)
    for at in range(per):
        down_keep[at] = grad_tile[down_rows(at, core), :]
        down_send[at] = grad_tile[down_rows(at, 1 - core), :]
    up_tile[...] = _dot(x_turn[...], upper_low).astype(jnp.bfloat16)
    for place in range(chips):
        up_keep[place] = up_tile[up_rows(place, core), :]
        up_send[place] = up_tile[up_rows(place, 1 - core), :]


def group_place(group, size):
    return lambda s, *t: (jnp.clip(s - group * size, 0, size - 1), 0, 0)


def feed_forward(table, x, g, bias, down, up, per=2):
    tokens, width = x.shape
    groups = len(down) // 2
    size, span, _ = down[0].shape
    owned = up[0].shape[1]
    inner = bias.shape[1]
    chips = groups * size
    tile = per * CORES * span
    whole = lambda s, t: (0, 0)
    column = lambda s, t: (0, t[s * per] // per)
    columns = lambda s, t: (0, 0, t[s * per] // per)
    down_spec = lambda place: pl.BlockSpec((per, span, width), place)
    up_spec = lambda count: pl.BlockSpec((count, owned, tile), columns)
    shape = jax.ShapeDtypeStruct
    return pl.pallas_call(
        functools.partial(feed_forward_kernel, groups, per),
        grid_spec=pltpu.PrefetchScalarGridSpec(
            num_scalar_prefetch=1,
            grid=(chips // per,),
            in_specs=[
                pl.BlockSpec((tokens, width), whole),
                pl.BlockSpec((tokens, width), whole),
                pl.BlockSpec((1, tile), column),
            ]
            + [down_spec(group_place(group, size // per)) for group in range(groups)] * 2
            + [up_spec(array.shape[0]) for array in up],
            out_specs=[
                pl.BlockSpec((tokens, width), whole),
                pl.BlockSpec((tokens, width), whole),
                down_spec(lambda s, t: (s, 0, 0)),
                down_spec(lambda s, t: (s, 0, 0)),
                up_spec(chips),
                up_spec(chips),
                pl.BlockSpec((1, tile), column),
            ],
            scratch_shapes=[
                pltpu.VMEM((width, tokens), jnp.bfloat16),
                pltpu.VMEM((width, tile), jnp.bfloat16),
                pltpu.VMEM((tile, width), jnp.bfloat16),
                pltpu.VMEM((tile, width), jnp.bfloat16),
            ],
        ),
        out_shape=[
            shape((tokens, width), jnp.float32),
            shape((tokens, width), jnp.float32),
            shape((chips, span, width), jnp.bfloat16),
            shape((chips, span, width), jnp.bfloat16),
            shape((chips, owned, inner), jnp.bfloat16),
            shape((chips, owned, inner), jnp.bfloat16),
            shape((1, inner), jnp.float32),
        ],
        compiler_params=pltpu.CompilerParams(vmem_limit_bytes=VMEM_BYTES),
        cost_estimate=estimate(45),
        name="feed_forward",
    )(table, x, g, bias, *down, *up)


def bits_of(size):
    return [1 << b for b in range(size.bit_length() - 1)]


def swap(value, step):
    axis, bit = step
    return lax.ppermute(value, axis, [(i, i ^ bit) for i in range(lax.axis_size(axis))])


def other_core(value):
    return swap(value, ("core", 1))


def offsets_of(steps, rings):
    found = [0]
    for axis, bit in steps:
        found = found + [o ^ (bit * rings if axis == "seq" else bit) for o in found]
    return found


def grow(value, steps):
    for step in steps:
        value = jnp.concatenate((value, swap(value, step)), axis=0)
    return value


def after(values, *others):
    values = tuple(values)
    return pl.pallas_call(
        lambda *refs: None,
        in_specs=[pl.BlockSpec(memory_space=pl.ANY)] * (len(values) + len(others)),
        out_specs=[pl.BlockSpec(memory_space=pl.ANY)] * len(values),
        out_shape=[jax.ShapeDtypeStruct(value.shape, value.dtype) for value in values],
        input_output_aliases={i: i for i in range(len(values))},
        name="after",
    )(*values, *others)


def widen(value, step):
    return jnp.stack((value, swap(value, step)), axis=1).reshape((-1,) + value.shape[1:])


def direct(value, axis):
    return [value] + [swap(value, (axis, m)) for m in range(1, lax.axis_size(axis))]


def add_low(left, right):
    return (left.astype(jnp.float32) + right.astype(jnp.float32)).astype(jnp.bfloat16)


def collect(groups, axis):
    total = groups[0].astype(jnp.float32)
    for m in range(1, len(groups)):
        total = total + swap(groups[m], (axis, m)).astype(jnp.float32)
    return total


def fold(total, axis):
    for bit in bits_of(total.shape[0]):
        pairs = total.reshape((total.shape[0] // 2, 2) + total.shape[1:])
        total = pairs[:, 0] + swap(pairs[:, 1].astype(jnp.bfloat16), (axis, bit)).astype(jnp.float32)
    return total[0]


def spread(blocks, axis):
    me = lax.axis_index(axis)
    out = jnp.zeros_like(blocks)
    for m in range(lax.axis_size(axis)):
        block = lax.dynamic_slice_in_dim(blocks, me ^ m, 1, 0)
        came = block if m == 0 else swap(block, (axis, m))
        out = lax.dynamic_update_slice_in_dim(out, came, me ^ m, 0)
    return out


def group_columns(weight, ways):
    rows = weight.shape[0]
    parts = weight.reshape(rows, 3, ways, -1, 2 * HEAD)
    return jnp.transpose(parts, (2, 0, 3, 1, 4)).reshape(ways, rows, -1)


def ungroup_columns(grouped):
    ways, rows, _ = grouped.shape
    parts = grouped.reshape(ways, rows, -1, 3, 2 * HEAD)
    return jnp.transpose(parts, (1, 3, 0, 2, 4)).reshape(rows, -1)


def pair_columns(bias, seq_index, ways):
    parts = bias.reshape(2, ways, -1, 2 * HEAD)
    mine = lax.dynamic_index_in_dim(parts, seq_index, 1, keepdims=False)
    return jnp.stack((mine[0], jnp.zeros_like(mine[0]), mine[1]), axis=1).reshape(-1)


def unpair_columns(sums, seq_index, ways):
    parts = sums.reshape(-1, 3, 2 * HEAD)
    mine = jnp.stack((parts[:, 0], parts[:, 2]))
    out = jnp.zeros((2, ways) + mine.shape[1:], jnp.float32)
    return lax.dynamic_update_slice_in_dim(out, mine[:, None], seq_index, 1).reshape(-1)


def norm_parts(values):
    centre = values - jnp.mean(values, axis=-1, keepdims=True)
    factor = lax.rsqrt(jnp.mean(centre * centre, axis=-1, keepdims=True) + EPSILON)
    return centre * factor, factor


def norm_back(grad, gain, unit, factor):
    turned = grad * gain
    inner = jnp.mean(turned * unit, axis=-1, keepdims=True)
    return factor * (turned - jnp.mean(turned, axis=-1, keepdims=True) - unit * inner)


def project_kernel(ways, table_ref, *refs):
    own_ref, one_ref, two_ref, low_ref, high_ref, w_ref, gain_ref, shift_ref, bias_ref = refs[:9]
    qkv_ref, normed_ref, unit_ref, weight_ref, rows = refs[-5:]
    cut = low_ref.shape[0]
    step = pl.program_id(0)
    copies = w_ref.shape[0]
    owned = weight_ref.shape[0] // (ways * copies)

    @pl.when(step == 0)
    def _():
        for place in range(copies):
            for sender in range(ways):
                start = (sender * copies + (table_ref[1] ^ place)) * owned
                weight_ref[pl.ds(pl.multiple_of(start, owned), owned), :] = w_ref[place, sender, :owned, :]

    for block, ref in enumerate((own_ref, one_ref, two_ref)):

        @pl.when(step == block)
        def _():
            rows[...] = ref[...]

    @pl.when(step == 3)
    def _():
        rows[:cut] = low_ref[...]
        rows[cut:] = high_ref[...]

    unit, _ = norm_parts(rows[...].astype(jnp.float32))
    normed = (unit * gain_ref[...] + shift_ref[...]).astype(jnp.bfloat16)
    unit_ref[...] = unit.astype(jnp.bfloat16)
    normed_ref[...] = normed
    qkv_ref[...] = (_dot(normed, weight_ref[...]) + bias_ref[...]).astype(jnp.bfloat16)


def project(table, blocks, packed, gain, shift, bias, ways, owned, deps=()):
    local, width = blocks[0].shape
    copies, _, _, triple = packed.shape
    whole = lambda s, t: (0, 0)
    place = lambda s, t: (t[0] ^ s, 0)
    full = lambda array: pl.BlockSpec(array.shape, lambda s, t: (0,) * array.ndim)
    operands = tuple(blocks) + (packed, gain, shift, bias)
    shape = jax.ShapeDtypeStruct
    length = ways * local
    return pl.pallas_call(
        functools.partial(project_kernel, ways),
        grid_spec=pltpu.PrefetchScalarGridSpec(
            num_scalar_prefetch=1,
            grid=(ways,),
            in_specs=[full(array) for array in operands]
            + [pl.BlockSpec(memory_space=pl.ANY)] * len(deps),
            out_specs=[
                pl.BlockSpec((local, triple), place),
                pl.BlockSpec((local, width), place),
                pl.BlockSpec((local, width), place),
                pl.BlockSpec((width, triple), whole),
            ],
            scratch_shapes=[pltpu.VMEM((local, width), jnp.bfloat16)],
        ),
        out_shape=[
            shape((length, triple), jnp.bfloat16),
            shape((length, width), jnp.bfloat16),
            shape((length, width), jnp.bfloat16),
            shape((width, triple), jnp.bfloat16),
        ],
        compiler_params=pltpu.CompilerParams(vmem_limit_bytes=VMEM_BYTES),
        cost_estimate=estimate(9),
        name="project",
    )(table, *operands, *deps)


def input_grad_kernel(low_ref, high_ref, w_ref, normed_ref, unit_ref, *refs):
    part_ref, weight_ref, sum_ref, bias_ref, total = refs[-5:]
    step = pl.program_id(0)

    @pl.when(step == 0)
    def _():
        total[...] = jnp.zeros_like(total)
        sum_ref[...] = jnp.zeros_like(sum_ref)
        bias_ref[...] = jnp.zeros_like(bias_ref)

    grad = jnp.concatenate((low_ref[...], high_ref[...]), axis=1)
    part = lax.dot_general(grad, w_ref[...], CONTRACT_LAST, preferred_element_type=jnp.float32)
    part_ref[...] = part.astype(jnp.bfloat16)
    total[...] += _dot(normed_ref[...].T, grad)
    sum_ref[0:1] += jnp.sum(part * unit_ref[...].astype(jnp.float32), axis=0, keepdims=True)
    sum_ref[1:2] += jnp.sum(part, axis=0, keepdims=True)
    bias_ref[0:1] += jnp.sum(grad.astype(jnp.float32), axis=0, keepdims=True)

    @pl.when(step == pl.num_programs(0) - 1)
    def _():
        weight_ref[...] = total[...].astype(jnp.bfloat16)


def input_grad(low, high, weight, normed, unit, deps=()):
    length, width = normed.shape
    triple = weight.shape[1]
    rows = 512
    block = lambda columns: pl.BlockSpec((rows, columns), lambda s: (s, 0))
    whole = lambda *size: pl.BlockSpec(size, lambda s: (0, 0))
    shape = jax.ShapeDtypeStruct
    return pl.pallas_call(
        input_grad_kernel,
        grid=(length // rows,),
        in_specs=[block(triple // 2), block(triple // 2), whole(width, triple), block(width), block(width)]
        + [pl.BlockSpec(memory_space=pl.ANY)] * len(deps),
        out_specs=[block(width), whole(width, triple), whole(8, width), whole(8, triple)],
        out_shape=[
            shape((length, width), jnp.bfloat16),
            shape((width, triple), jnp.bfloat16),
            shape((8, width), jnp.float32),
            shape((8, triple), jnp.float32),
        ],
        scratch_shapes=[pltpu.VMEM((width, triple), jnp.float32)],
        compiler_params=pltpu.CompilerParams(vmem_limit_bytes=VMEM_BYTES),
        cost_estimate=estimate(10),
        name="input_grad",
    )(low, high, weight, normed, unit, *deps)


def output_rows(table_ref, place, who, owned):
    start = table_ref[place] * (CORES * owned) + who * owned
    return pl.ds(pl.multiple_of(start, owned), owned)


def join_groups(ref):
    return jnp.concatenate([ref[s] for s in range(ref.shape[0])], axis=1)


def output_kernel(table_ref, context_ref, x_ref, bias_ref, gain_ref, shift_ref, *refs):
    residual_ref, normed_ref, weight_ref = refs[-3:]
    parts = refs[:-3]
    groups = len(parts) // 2
    size, owned, _ = parts[0].shape
    core = table_ref[2 * groups * size]

    @pl.when(pl.program_id(0) == 0)
    def _():
        for place in range(groups * size):
            group, at = divmod(place, size)
            weight_ref[output_rows(table_ref, groups * size + place, core, owned), :] = parts[group][at]
            weight_ref[output_rows(table_ref, groups * size + place, 1 - core, owned), :] = parts[groups + group][at]

    branch = _dot(join_groups(context_ref), weight_ref[...]) + bias_ref[...]
    residual = x_ref[...].astype(jnp.float32) + branch
    residual_ref[...] = residual
    unit, _ = norm_parts(residual)
    normed_ref[...] = (unit * gain_ref[...] + shift_ref[...]).astype(jnp.bfloat16)


def project_output(table, context, parts, x, bias, gain, shift):
    local, width = x.shape
    ways = context.shape[0]
    rows = 256
    vector = pl.BlockSpec((1, width), lambda s, t: (0, 0))
    block = pl.BlockSpec((rows, width), lambda s, t: (s, 0))
    heads = pl.BlockSpec((ways, rows, width // ways), lambda s, t: (0, s, 0))
    size, owned, total = parts[0].shape
    weight = pl.BlockSpec((size, owned, width), lambda s, t: (0, 0, total // width - 1))
    shape = jax.ShapeDtypeStruct
    return pl.pallas_call(
        output_kernel,
        grid_spec=pltpu.PrefetchScalarGridSpec(
            num_scalar_prefetch=1,
            grid=(local // rows,),
            in_specs=[heads, block, vector, vector, vector] + [weight] * len(parts),
            out_specs=[block, block, pl.BlockSpec((width, width), lambda s, t: (0, 0))],
        ),
        out_shape=[
            shape((local, width), jnp.float32),
            shape((local, width), jnp.bfloat16),
            shape((width, width), jnp.bfloat16),
        ],
        compiler_params=pltpu.CompilerParams(vmem_limit_bytes=VMEM_BYTES),
        cost_estimate=estimate(5),
        name="project_output",
    )(table, context, x, bias, gain, shift, *parts)


def residual_kernel(table_ref, grad_ref, residual_ref, up_ref, context_ref, w_ref, gain_ref, *refs):
    out_ref, context_grad_ref, keep_ref, send_ref, sum_ref, total, held = refs[-7:]
    step = pl.program_id(0)
    chips, owned, _ = keep_ref.shape
    ways = context_ref.shape[0]
    core = table_ref[2 * chips]

    @pl.when(step == 0)
    def _():
        total[...] = jnp.zeros_like(total)
        sum_ref[...] = jnp.zeros_like(sum_ref)

    unit, factor = norm_parts(residual_ref[...])
    grad = grad_ref[...]
    upstream = up_ref[...].astype(jnp.float32)
    through = upstream + norm_back(grad, gain_ref[...], unit, factor)
    out_ref[...] = through
    branch = through.astype(jnp.bfloat16)
    context_grad = lax.dot_general(
        branch, w_ref[...], CONTRACT_LAST, preferred_element_type=jnp.float32
    ).astype(jnp.bfloat16)
    wide = context_grad.shape[1] // ways
    for s in range(ways):
        context_grad_ref[s] = context_grad[:, s * wide : (s + 1) * wide]
    total[...] += _dot(join_groups(context_ref).T, branch)
    for row, term in enumerate((grad * unit, grad, through, upstream)):
        sum_ref[row : row + 1] += jnp.sum(term, axis=0, keepdims=True)

    @pl.when(step == pl.num_programs(0) - 1)
    def _():
        held[...] = total[...].astype(jnp.bfloat16)
        for place in range(chips):
            keep_ref[place] = held[output_rows(table_ref, place, core, owned), :]
            send_ref[place] = held[output_rows(table_ref, place, 1 - core, owned), :]


def residual_grad(table, grad, residual, upstream, context, weight, gain, chips):
    local, width = residual.shape
    ways = context.shape[0]
    rows = 256
    owned = width // (chips * CORES)
    whole = lambda *size: pl.BlockSpec(size, lambda s, t: (0,) * len(size))
    block = pl.BlockSpec((rows, width), lambda s, t: (s, 0))
    heads = pl.BlockSpec((ways, rows, width // ways), lambda s, t: (0, s, 0))
    shape = jax.ShapeDtypeStruct
    return pl.pallas_call(
        residual_kernel,
        grid_spec=pltpu.PrefetchScalarGridSpec(
            num_scalar_prefetch=1,
            grid=(local // rows,),
            in_specs=[block, block, block, heads, whole(width, width), whole(1, width)],
            out_specs=[block, heads, whole(chips, owned, width), whole(chips, owned, width), whole(8, width)],
            scratch_shapes=[pltpu.VMEM((width, width), jnp.float32), pltpu.VMEM((width, width), jnp.bfloat16)],
        ),
        out_shape=[
            shape((local, width), jnp.float32),
            shape((ways, local, width // ways), jnp.bfloat16),
            shape((chips, owned, width), jnp.bfloat16),
            shape((chips, owned, width), jnp.bfloat16),
            shape((8, width), jnp.float32),
        ],
        compiler_params=pltpu.CompilerParams(vmem_limit_bytes=VMEM_BYTES),
        cost_estimate=estimate(7),
        name="residual_grad",
    )(table, grad, residual, upstream, context, weight, gain)


def meet_kernel(groups, up_groups, down_keep, down_came, output_keep, output_came, up_keep, up_came, *refs):
    step = pl.program_id(0)
    steps = pl.num_programs(0)
    span = down_keep.shape[1]

    def both(left, right):
        return (left[...].astype(jnp.float32) + right[...].astype(jnp.float32)).astype(jnp.bfloat16)

    for group in range(groups):

        @pl.when(step // (steps // groups) == group)
        def _():
            refs[group][:, :span] = both(down_keep, down_came)
            refs[group][:, span:] = both(output_keep, output_came)

    for group in range(up_groups):

        @pl.when(step // (steps // up_groups) == group)
        def _():
            refs[groups + group][...] = both(up_keep, up_came)


def meet(down_keep, down_came, output_keep, output_came, up_keep, up_came, groups, up_groups, per=2):
    chips, span, width = down_keep.shape
    owned, inner = up_keep.shape[1:]
    block = lambda rows, columns: pl.BlockSpec((per, rows, columns), lambda s: (s, 0, 0))
    parts = [(span + owned, width, chips // groups, group) for group in range(groups)]
    parts += [(owned, inner, chips // up_groups, group) for group in range(up_groups)]
    outs = [pl.BlockSpec((per, rows, columns), group_place(group, size // per)) for rows, columns, size, group in parts]
    shapes = [jax.ShapeDtypeStruct((size, rows, columns), jnp.bfloat16) for rows, columns, size, _ in parts]
    return pl.pallas_call(
        functools.partial(meet_kernel, groups, up_groups),
        grid=(chips // per,),
        in_specs=[block(span, width)] * 2 + [block(owned, width)] * 2 + [block(owned, inner)] * 2,
        out_specs=outs,
        out_shape=shapes,
        compiler_params=pltpu.CompilerParams(vmem_limit_bytes=VMEM_BYTES),
        cost_estimate=estimate(9),
        name="meet",
    )(down_keep, down_came, output_keep, output_came, up_keep, up_came)


def halve(value, step, kind):
    axis, bit = step
    mine = (lax.axis_index(axis) // bit) % 2
    sent = lax.dynamic_index_in_dim(value, 1 - mine, 0, keepdims=False).astype(kind)
    kept = lax.dynamic_index_in_dim(value, mine, 0, keepdims=False)
    return kept.astype(jnp.float32) + swap(sent, step).astype(jnp.float32)


def scatter_copies(value, kind):
    rings = lax.axis_size("ring")
    value = jnp.moveaxis(value.reshape((rings, CORES) + value.shape[1:]), 1, 0)
    value = halve(value, ("core", 1), kind)
    for bit in bits_of(rings):
        shape = value.shape
        value = jnp.moveaxis(value.reshape((shape[0] // 2, 2) + shape[1:]), 1, 0)
        value = halve(value, ("ring", bit), kind)
    return value[0]


def scatter_seq(value, kind):
    for bit in reversed(bits_of(lax.axis_size("seq"))):
        value = halve(value.reshape((2, value.shape[0] // 2) + value.shape[1:]), ("seq", bit), kind)
    return value[0]


def layer_norm(values, norm_gain, norm_shift):
    centre = values - jnp.mean(values, axis=-1, keepdims=True)
    spread = jnp.mean(centre * centre, axis=-1, keepdims=True)
    return centre * lax.rsqrt(spread + EPSILON) * norm_gain + norm_shift


def tanh_gelu(upper_in):
    return jax.nn.gelu(upper_in, approximate=True)


def gather_small(parts):
    sizes = [part.shape[0] for part in parts]
    width = -(-sum(sizes) // 512) * 512
    packed = jnp.concatenate(list(parts) + [jnp.zeros((width - sum(sizes),), parts[0].dtype)])
    whole = lax.all_gather(packed.reshape(4, width // 4), WORLD, axis=0, tiled=False)
    whole = whole.reshape(-1, width).astype(jnp.float32)
    out, start = [], 0
    for size in sizes:
        out.append(whole[:, start : start + size].reshape(-1))
        start += size
    return out


def scatter_small(parts, world):
    rows = [part.reshape(world, -1) for part in parts]
    sizes = [row.shape[1] for row in rows]
    width = -(-sum(sizes) // 128) * 128
    packed = jnp.concatenate(rows + [jnp.zeros((world, width - sum(sizes)), jnp.float32)], axis=1)
    owned = lax.psum_scatter(packed, WORLD, scatter_dimension=0, tiled=True)[0]
    out, start = [], 0
    for size in sizes:
        out.append(owned[start : start + size])
        start += size
    return out


def gather_weight(shard):
    mine = lax.all_gather(shard, CHIPS, axis=0, tiled=False)
    theirs = other_core(mine)
    first = lax.axis_index("core") == 0
    pair = jnp.stack((jnp.where(first, mine, theirs), jnp.where(first, theirs, mine)), axis=1)
    return pair.reshape(-1, shard.shape[-1])


def pick_rows(columns, chips, core):
    tokens, width = columns.shape
    parts = columns.reshape(tokens, chips, CORES, width // (chips * CORES))
    return lax.dynamic_index_in_dim(parts, core, 2, keepdims=False).reshape(tokens, width // CORES)


def contract_tokens(left, right):
    return lax.dot_general(left, right, (((0,), (0,)), ((), ())), preferred_element_type=jnp.float32)


def scatter_weight_grad(left, right, chips):
    core = lax.axis_index("core")
    sent = contract_tokens(pick_rows(left, chips, 1 - core), right).astype(jnp.bfloat16)
    came = other_core(sent).astype(jnp.float32)
    both = (contract_tokens(pick_rows(left, chips, core), right) + came).astype(jnp.bfloat16)
    return lax.psum_scatter(both, CHIPS, scatter_dimension=0, tiled=True).astype(jnp.float32)


def plain_body(
    tokens_in,
    out_grad,
    first_gain,
    first_shift,
    input_weight,
    input_bias,
    output_weight,
    output_bias,
    second_gain,
    second_shift,
    up_weight,
    up_bias,
    down_weight,
    down_bias,
):
    ways = lax.axis_size("seq")
    rings = lax.axis_size("ring")
    chips = ways * rings
    model_width = tokens_in.shape[-1]
    group_width = model_width // ways
    head_group = group_width // HEAD
    rows_in = tokens_in.reshape(-1, model_width)
    local = rows_in.shape[0]
    length = local * ways
    upstream = out_grad.reshape(local, model_width)

    (
        gain_first,
        shift_first,
        bias_input,
        bias_output,
        gain_second,
        shift_second,
        bias_up,
        bias_down,
    ) = gather_small(
        (first_gain, first_shift, input_bias, output_bias, second_gain, second_shift, up_bias, down_bias)
    )
    seq_index = lax.axis_index("seq")

    all_rows = lax.all_gather(rows_in, "seq", axis=0, tiled=True)
    owned_rows = input_weight.shape[0]
    by_group = group_columns(input_weight, ways)
    columns = lax.all_to_all(by_group, "seq", split_axis=0, concat_axis=0, tiled=True)
    columns = lax.all_gather(columns, ("ring", "core"), axis=0, tiled=False)
    weight_input = jnp.moveaxis(columns, 0, 1).reshape(model_width, 3 * group_width)

    weight_output = gather_weight(output_weight)
    weight_up = gather_weight(up_weight)
    weight_down = gather_weight(down_weight)

    normed = layer_norm(all_rows.astype(jnp.float32), gain_first, shift_first).astype(jnp.bfloat16)
    bias_group = pair_columns(bias_input, seq_index, ways)
    qkv = (jnp.dot(normed, weight_input, preferred_element_type=jnp.float32) + bias_group).astype(
        jnp.bfloat16
    )
    head_ids = (seq_index * head_group + jnp.arange(head_group, dtype=jnp.int32)).astype(jnp.float32)
    slopes = jnp.exp2(-8.0 * (head_ids + 1.0) / HEADS)
    pairs = range(head_group // 2)
    kept = [attend_forward(slopes[2 * p : 2 * p + 2], qkv, p) for p in pairs]
    context_split = jnp.concatenate([k[0] for k in kept], axis=1)
    context = lax.all_to_all(
        context_split.reshape(ways, local, group_width), "seq", split_axis=0, concat_axis=0, tiled=True
    )
    context = jnp.moveaxis(context, 0, 1).reshape(local, model_width)

    inputs = rows_in.astype(jnp.float32)
    branch = jnp.dot(context, weight_output, preferred_element_type=jnp.float32) + bias_output
    residual = inputs + branch
    normed_two_float, second_back = jax.vjp(layer_norm, residual, gain_second, shift_second)
    normed_two = normed_two_float.astype(jnp.bfloat16)
    upper = jnp.dot(normed_two, weight_up, preferred_element_type=jnp.float32) + bias_up
    activated, gelu_back = jax.vjp(tanh_gelu, upper)
    hidden = activated.astype(jnp.bfloat16)
    layer_out = (
        residual + jnp.dot(hidden, weight_down, preferred_element_type=jnp.float32) + bias_down
    ).astype(jnp.bfloat16)
    grad_hidden = lax.dot_general(
        upstream, weight_down, (((1,), (1,)), ((), ())), preferred_element_type=jnp.float32
    )
    grad_upper = gelu_back(grad_hidden)[0]
    upper_low = grad_upper.astype(jnp.bfloat16)
    grad_normed_two = lax.dot_general(
        upper_low, weight_up, (((1,), (1,)), ((), ())), preferred_element_type=jnp.float32
    )
    grad_through, grad_second_gain, grad_second_shift = second_back(grad_normed_two)
    grad_residual = upstream.astype(jnp.float32) + grad_through
    branch_low = grad_residual.astype(jnp.bfloat16)
    context_grad = lax.dot_general(
        branch_low, weight_output, (((1,), (1,)), ((), ())), preferred_element_type=jnp.float32
    ).astype(jnp.bfloat16)
    grad_split = jnp.moveaxis(context_grad.reshape(local, ways, group_width), 1, 0)
    grad_split = lax.all_to_all(grad_split, "seq", split_axis=0, concat_axis=0, tiled=True)
    grad_split = grad_split.reshape(length, group_width)

    grad_down_weight = scatter_weight_grad(hidden, upstream, chips)
    grad_up_weight = scatter_weight_grad(normed_two, upper_low, chips)
    grad_output_weight = scatter_weight_grad(context, branch_low, chips)

    grad_qkv = jnp.concatenate(
        [
            attend_backward(
                slopes[2 * p : 2 * p + 2], qkv, grad_split, kept[p][1], kept[p][2], p
            )
            for p in pairs
        ],
        axis=1,
    )

    grad_normed = lax.dot_general(
        grad_qkv, weight_input, (((1,), (1,)), ((), ())), preferred_element_type=jnp.float32
    ).astype(jnp.bfloat16)
    grad_normed = lax.all_to_all(
        grad_normed.reshape(ways, local, model_width), "seq", split_axis=0, concat_axis=0, tiled=True
    )
    grad_normed = jnp.sum(grad_normed.astype(jnp.float32), axis=0)

    grad_columns = contract_tokens(normed, grad_qkv)
    grad_columns = jnp.moveaxis(
        grad_columns.reshape(ways, rings * CORES, owned_rows, 3 * group_width), 1, 0
    ).astype(jnp.bfloat16)
    grad_columns = lax.psum_scatter(
        grad_columns.reshape(-1, 3 * group_width), ("ring", "core"), scatter_dimension=0, tiled=True
    )
    grad_columns = lax.all_to_all(
        grad_columns.reshape(ways, owned_rows, 3 * group_width), "seq", split_axis=0, concat_axis=0, tiled=True
    )
    grad_input_weight = ungroup_columns(grad_columns).astype(jnp.float32)
    grad_input_bias = unpair_columns(jnp.sum(grad_qkv.astype(jnp.float32), axis=0), seq_index, ways)
    _, first_back = jax.vjp(layer_norm, inputs, gain_first, shift_first)
    grad_entry, grad_first_gain, grad_first_shift = first_back(grad_normed)
    tokens_grad = grad_residual + grad_entry

    small = scatter_small(
        (
            grad_first_gain,
            grad_first_shift,
            grad_input_bias,
            jnp.sum(grad_residual, axis=0),
            grad_second_gain,
            grad_second_shift,
            jnp.sum(grad_upper, axis=0),
            jnp.sum(upstream.astype(jnp.float32), axis=0),
        ),
        chips * CORES,
    )
    return (
        layer_out.reshape(tokens_in.shape),
        tokens_grad.reshape(tokens_in.shape),
        small[0],
        small[1],
        grad_input_weight,
        small[2],
        grad_output_weight,
        small[3],
        small[4],
        small[5],
        grad_up_weight,
        small[6],
        grad_down_weight,
        small[7],
    )


def blocked_body(
    tokens_in,
    out_grad,
    first_gain,
    first_shift,
    input_weight,
    input_bias,
    output_weight,
    output_bias,
    second_gain,
    second_shift,
    up_weight,
    up_bias,
    down_weight,
    down_bias,
):
    ways = lax.axis_size("seq")
    rings = lax.axis_size("ring")
    chips = ways * rings
    copies = rings * CORES
    world = chips * CORES
    model_width = tokens_in.shape[-1]
    head_group = model_width // ways // HEAD
    rows_in = tokens_in.reshape(-1, model_width)
    local = rows_in.shape[0]
    length = local * ways
    upstream = out_grad.reshape(local, model_width)
    seq_index = lax.axis_index("seq")
    core = lax.axis_index("core")
    chip_index = seq_index * rings + lax.axis_index("ring")
    copy_index = lax.axis_index("ring") * CORES + core

    ring = lax.axis_index("ring")
    far_bit, near_bit = rings // 2, 1
    down_away = [s * rings + r for s in range(ways) for r in range(rings)]
    up_away = [s * rings + near + far for near in (0, near_bit) for s in range(ways) for far in (0, far_bit)]
    down_table, up_table = (jnp.array(away, jnp.int32) ^ chip_index for away in (down_away, up_away))
    table = jnp.concatenate((down_table, up_table, core[None]))

    vectors = (first_gain, first_shift, input_bias, output_bias, second_gain, second_shift, up_bias, down_bias)
    sizes = [vector.shape[0] for vector in vectors]
    owned = input_weight.shape[0]
    by_group = group_columns(input_weight, ways)
    triple = by_group.shape[-1]
    packed = jnp.concatenate([jnp.pad(vector, (0, 128 - vector.shape[0]))[None] for vector in vectors])
    packed = jnp.pad(packed, ((0, 8 - len(sizes)), (0, triple - 128)))
    by_group = jnp.concatenate((by_group, jnp.broadcast_to(packed[None], (ways, 8, triple))), axis=1)
    up_shard = jnp.concatenate((up_weight, output_weight), axis=1)
    seq_steps = [("seq", bit) for bit in bits_of(ways)]
    one, two = (swap(rows_in, step) for step in seq_steps)
    up_one = widen(up_shard[None], ("ring", far_bit))
    (by_group,) = after((by_group,), up_one)
    (grouped,) = after((spread(by_group, "seq"),), one, two)
    cut = local // 2
    low, high = swap(two[:cut], seq_steps[0]), swap(one[cut:], seq_steps[1])
    blocks = (rows_in, one, two, low, high)
    columns = grouped[None]
    for bit in (far_bit, near_bit):
        columns = widen(columns, ("ring", bit))
        if bit == far_bit:
            (columns,) = after((columns,), low, high)
            (down_one,) = after((down_weight[None],), columns)
    for bit in (far_bit, near_bit):
        down_one = widen(down_one, ("ring", bit))
    columns = jnp.stack((columns, other_core(columns)), axis=1).reshape((copies,) + by_group.shape)
    found = columns[:, :, owned : owned + len(sizes), :128].reshape(world, -1)
    here = jnp.arange(world, dtype=jnp.int32)
    wanted = ((here % copies) ^ copy_index) * ways + here // copies
    pick = (wanted[:, None] == here[None, :]).astype(jnp.bfloat16)
    found = jnp.dot(pick, found, preferred_element_type=jnp.float32)
    vectors = [found[:, 128 * i : 128 * i + size].reshape(1, -1) for i, size in enumerate(sizes)]
    gain_first, shift_first, bias_input, bias_output, gain_second, shift_second, bias_up, bias_down = vectors
    bias_group = pair_columns(bias_input[0], seq_index, ways)[None]


    (up_one,) = after((up_one,), low, high)
    up_near = jnp.concatenate(direct(up_one, "seq"))
    (down_one,) = after((down_one,), up_near)
    (up_near,) = after((up_near,), columns, down_one)
    down_mine = direct(down_one, "seq")
    up_far = swap(up_near, ("ring", near_bit))

    places = jnp.stack((seq_index, copy_index)).astype(jnp.int32)
    qkv, normed, unit, weight_input = project(
        places, blocks, columns, gain_first, shift_first, bias_group, ways, owned
    )
    head_ids = (seq_index * head_group + jnp.arange(head_group, dtype=jnp.int32)).astype(jnp.float32)
    slopes = jnp.exp2(-8.0 * (head_ids + 1.0) / HEADS)

    def exchange(value):
        return lax.all_to_all(
            value.reshape(ways, local, -1), "seq", split_axis=0, concat_axis=0, tiled=True
        )

    swapped = other_core(up_near)
    kept, contexts, done = [], [], (down_one, up_near)
    for pair in range(2):
        context, wide, log_totals = attend_forward(slopes[2 * pair : 2 * pair + 2], qkv, pair, done)
        kept.append((wide, log_totals))
        contexts.append(context)
        done = (log_totals, swapped)
    context = exchange(jnp.concatenate(contexts, axis=1))

    late = list(after([up_far] + down_mine, context))
    theirs = [other_core(group) for group in late]
    down = late[1:] + theirs[1:]
    up = [up_near, late[0], swapped, theirs[0]]
    residual, normed_two, weight_output = project_output(
        table, context, up, rows_in, bias_output, gain_second, shift_second
    )
    layer, grad_normed_two, down_keep, down_send, up_keep, up_send, grad_up_bias = feed_forward(
        table, normed_two, upstream, bias_up, down, up
    )
    grad_residual, context_grad, output_keep, output_send, middle_sums = residual_grad(
        table, grad_normed_two, residual, upstream, context, weight_output, gain_second, chips
    )

    context_grad = exchange(context_grad).reshape(length, -1)
    met = list(
        meet(down_keep, other_core(down_send), output_keep, other_core(output_send), up_keep, other_core(up_send), ways, 2)
    )
    met = list(after(met, context_grad))
    came = [swap(met[m], ("seq", m)) for m in range(1, ways)] + [swap(met[ways + 1], ("ring", near_bit))]

    grads, ready = [], [met[0], met[ways]]
    for pair in range(2):
        grads.append(attend_backward(slopes[2 * pair : 2 * pair + 2], qkv, context_grad, *kept[pair], pair, ready))
        ready = [grads[0]]
    (up_came,) = after(came[ways - 1 :], grads[1])
    up_sum = (met[ways].astype(jnp.float32) + up_came.astype(jnp.float32)).astype(jnp.bfloat16)
    up_sum = up_sum.reshape((ways, 2) + up_sum.shape[1:])
    down_sum = met[0].astype(jnp.float32)
    for group in after(came[: ways - 1], up_sum):
        down_sum = down_sum + group.astype(jnp.float32)

    part, grad_columns, first_sums, bias_sums = input_grad(
        grads[0], grads[1], weight_input, normed, unit, (down_sum, up_sum)
    )
    up_came = [swap(up_sum[m], ("seq", m)) for m in range(1, ways)]
    down_sum = down_sum.reshape((2, 2) + down_sum.shape[1:])
    down_came = swap(down_sum[:, 1].astype(jnp.bfloat16), ("ring", near_bit))
    down_sum = down_sum[:, 0] + down_came.astype(jnp.float32)
    sums = (
        first_sums[0],
        first_sums[1],
        unpair_columns(bias_sums[0], seq_index, ways),
        middle_sums[2],
        middle_sums[0],
        middle_sums[1],
        grad_up_bias[0],
        middle_sums[3],
    )
    rows = [jnp.pad(term.reshape(world, -1), ((0, 0), (0, 128 - size))) for term, size in zip(sums, sizes)]
    rows = jnp.stack(rows, axis=1).astype(jnp.bfloat16)
    rows = jnp.pad(rows, ((0, 0), (0, 8 - len(sizes)), (0, triple - 128)))
    both = jnp.concatenate((grad_columns.reshape(world, owned, triple), rows), axis=1)
    both = both.reshape(ways, rings, CORES, owned + 8, triple)
    came = other_core(lax.dynamic_index_in_dim(both, 1 - core, 2, keepdims=False))
    (came,) = after((came,), *up_came, down_came)
    both = lax.dynamic_index_in_dim(both, core, 2, keepdims=False).astype(jnp.float32) + came.astype(jnp.float32)
    ring = lax.axis_index("ring")
    both = jnp.stack([lax.dynamic_index_in_dim(both, ring ^ m, 1, keepdims=False) for m in range(rings)])
    up_sum = up_sum[0].astype(jnp.float32)
    for group in up_came:
        up_sum = up_sum + group.astype(jnp.float32)
    grad_normed = jnp.sum(exchange(part).astype(jnp.float32), axis=0)
    inputs = rows_in.astype(jnp.float32)
    tokens_grad = grad_residual + norm_back(grad_normed, gain_first, *norm_parts(inputs))

    (layer,) = after((layer,), both)
    layer_out = (residual + layer + bias_down).astype(jnp.bfloat16)
    both = fold(both, "ring").astype(jnp.bfloat16)
    down_low, up_low = after([value[1].astype(jnp.bfloat16) for value in (down_sum, up_sum)], both)
    down_came, up_came = swap(down_low, ("ring", far_bit)), swap(up_low, ("ring", far_bit))
    both = spread(both, "seq")
    down_came, up_came = after((down_came, up_came), tokens_grad)
    down_sum = down_sum[0] + down_came.astype(jnp.float32)
    grad_up_weight = up_sum[0] + up_came.astype(jnp.float32)
    grad_down_weight, grad_output_weight = down_sum[: down_weight.shape[0]], down_sum[down_weight.shape[0] :]
    wide = 2 * HEAD
    grad_input_weight = jnp.concatenate(
        [
            both[sender, :owned, (3 * pair + part) * wide : (3 * pair + part + 1) * wide]
            for part in range(3)
            for sender in range(ways)
            for pair in range(head_group // 2)
        ],
        axis=1,
    ).astype(jnp.float32)
    rows = jnp.sum(both[:, owned:, :128].astype(jnp.float32), axis=0)
    small = [rows[i, :size] for i, size in enumerate(sizes)]
    return (
        layer_out.reshape(tokens_in.shape),
        tokens_grad.reshape(tokens_in.shape),
        small[0],
        small[1],
        grad_input_weight,
        small[2],
        grad_output_weight,
        small[3],
        small[4],
        small[5],
        grad_up_weight,
        small[6],
        grad_down_weight,
        small[7],
    )


def solution(mesh):
    ways, copies = mesh.shape["seq"], mesh.shape["dp"]
    split = Mesh(mesh.devices.reshape(ways, copies // CORES, CORES), WORLD)
    token = P(("ring", "core"), "seq", None)
    vector = P(WORLD)
    matrix = P(WORLD, None)
    weights = (vector, vector, matrix, vector, matrix, vector, vector, vector, matrix, vector, matrix, vector)
    step = blocked_body if ways == 4 else plain_body
    return jax.shard_map(
        step,
        mesh=split,
        in_specs=(token, token) + weights,
        out_specs=(token, token) + weights,
        check_vma=False,
    )
```

```python
import functools
import math

import jax
import jax.numpy as jnp
from jax import lax
from jax.experimental import pallas as pl
from jax.experimental.pallas import tpu as pltpu
from jax.sharding import Mesh
from jax.sharding import PartitionSpec as P

HEADS = 16
HEAD = 64
EPSILON = 1e-05
LOG2E = math.log2(math.e)
TILE = 256
VMEM_BYTES = 60 * 1024 * 1024
CORES = 2
CHIPS = ("seq", "ring")
WORLD = ("seq", "ring", "core")

def _dot(a, b):
    return jnp.dot(a, b, preferred_element_type=jnp.float32)

def _bias_tile(slope):
    return lax.broadcasted_iota(jnp.int32, (TILE, TILE), 0).astype(jnp.float32) * slope

def _keep():
    return lax.broadcasted_iota(jnp.int32, (TILE, TILE), 0) <= lax.broadcasted_iota(jnp.int32, (TILE, TILE), 1)

def _row_mask(shape, axis, half):
    ids = lax.broadcasted_iota(jnp.int32, shape, axis)
    return (ids >= HEAD) == (half == 1)

def estimate(micros):
    return pl.CostEstimate(flops=int(micros * 1e8), bytes_accessed=0, transcendentals=0)

def forward_kernel(slope_ref, q_ref, k_ref, v_ref, *refs):
    ctx_ref, wide_ref, log_ref, q_turn, v_turn, scores = refs[-6:]
    head = pl.program_id(0)
    half = lax.rem(head, 2)
    length = q_ref.shape[0]
    tiles = length // TILE

    @pl.when(half == 0)
    def _():
        q_turn[...] = q_ref[...].T
        v_turn[...] = v_ref[...].T

    slope = slope_ref[head] * LOG2E
    scale = HEAD ** -0.5 * LOG2E
    rows = pl.ds(pl.multiple_of(half * HEAD, HEAD), HEAD)
    bias = _bias_tile(slope)
    for i in range(tiles):
        cols = slice(i * TILE, (i + 1) * TILE)
        q_block = q_turn[:, cols]
        q_block = jnp.where(_row_mask(q_block.shape, 0, half), q_block, jnp.zeros_like(q_block))
        peak = None
        for c in range(i + 1):
            part = _dot(k_ref[c * TILE:(c + 1) * TILE, :], q_block) * scale + bias
            if c == i:
                part = jnp.where(_keep(), part, -jnp.inf)
            scores[i % 2, c] = part
            top = jnp.max(part, axis=0, keepdims=True) + slope * ((c - i) * TILE)
            peak = top if peak is None else jnp.maximum(peak, top)
        total = jnp.zeros((1, TILE), jnp.float32)
        out = jnp.zeros((HEAD, TILE), jnp.float32)
        for c in range(i + 1):
            probs = jnp.exp2(scores[i % 2, c] - (peak - slope * ((c - i) * TILE)))
            total = total + jnp.sum(probs, axis=0, keepdims=True)
            out = out + _dot(v_turn[rows, c * TILE:(c + 1) * TILE], probs.astype(jnp.bfloat16))
        wide_ref[rows, cols] = out / total
        log_ref[:, cols] = jnp.broadcast_to(peak + jnp.log2(total), (8, TILE))

    @pl.when(half == 1)
    def _():
        ctx_ref[...] = wide_ref[...].T.astype(jnp.bfloat16)

def attend_forward(slopes, qkv, pair, deps=()):
    length = qkv.shape[0]
    spec = lambda part: pl.BlockSpec((length, 2 * HEAD), lambda h: (0, 3 * pair + part))
    return pl.pallas_call(
        forward_kernel,
        grid=(2,),
        in_specs=[pl.BlockSpec(memory_space=pltpu.SMEM), spec(0), spec(1), spec(2)]
        + [pl.BlockSpec(memory_space=pl.ANY)] * len(deps),
        out_specs=[
            pl.BlockSpec((length, 2 * HEAD), lambda h: (0, 0)),
            pl.BlockSpec((2 * HEAD, length), lambda h: (0, 0)),
            pl.BlockSpec((8, length), lambda h: (h, 0)),
        ],
        out_shape=[
            jax.ShapeDtypeStruct((length, 2 * HEAD), jnp.bfloat16),
            jax.ShapeDtypeStruct((2 * HEAD, length), jnp.float32),
            jax.ShapeDtypeStruct((2 * 8, length), jnp.float32),
        ],
        scratch_shapes=[
            pltpu.VMEM((2 * HEAD, length), jnp.bfloat16),
            pltpu.VMEM((2 * HEAD, length), jnp.bfloat16),
            pltpu.VMEM((2, length // TILE, TILE, TILE), jnp.float32),
        ],
        compiler_params=pltpu.CompilerParams(vmem_limit_bytes=VMEM_BYTES),
        cost_estimate=estimate(10.5),
        name="attend_forward",
    )(slopes, qkv, qkv, qkv, *deps)

def backward_kernel(slope_ref, q_ref, k_ref, v_ref, g_ref, wide_ref, log_ref, *refs):
    out_ref, q_turn, k_turn, g_turn, dq_turn, dk_sum, dv_sum = refs[-7:]
    head = pl.program_id(0)
    half = lax.rem(head, 2)
    length = q_ref.shape[0]
    tiles = length // TILE
    wide = 2 * HEAD

    @pl.when(half == 0)
    def _():
        q_turn[...] = q_ref[...].T
        k_turn[...] = k_ref[...].T
        g_turn[...] = g_ref[...].T

    slope = slope_ref[head] * LOG2E
    scale = HEAD ** -0.5 * LOG2E
    rows = pl.ds(pl.multiple_of(half * HEAD, HEAD), HEAD)
    bias = _bias_tile(slope)
    inner = jnp.sum(wide_ref[rows, :] * g_turn[rows, :].astype(jnp.float32), axis=0, keepdims=True)
    for c in range(tiles):
        span = slice(c * TILE, (c + 1) * TILE)
        dk = jnp.zeros((TILE, 2 * HEAD), jnp.float32)
        dv = jnp.zeros((TILE, 2 * HEAD), jnp.float32)
        for i in range(c, tiles):
            cols = slice(i * TILE, (i + 1) * TILE)
            q_cols = q_turn[:, cols]
            q_cols = jnp.where(_row_mask(q_cols.shape, 0, half), q_cols, jnp.zeros_like(q_cols))
            g_cols = g_turn[:, cols]
            g_cols = jnp.where(_row_mask(g_cols.shape, 0, half), g_cols, jnp.zeros_like(g_cols))
            q_rows = q_ref[cols, :]
            q_rows = jnp.where(_row_mask(q_rows.shape, 1, half), q_rows, jnp.zeros_like(q_rows))
            g_rows = g_ref[cols, :]
            g_rows = jnp.where(_row_mask(g_rows.shape, 1, half), g_rows, jnp.zeros_like(g_rows))
            part = _dot(k_ref[span, :], q_cols) * scale + bias
            if c == i:
                part = jnp.where(_keep(), part, -jnp.inf)
            probs = jnp.exp2(part - (log_ref[0:1, cols] - slope * ((c - i) * TILE)))
            grad = (probs * (_dot(v_ref[span, :], g_cols) - inner[:, cols])).astype(jnp.bfloat16)
            dv = dv + _dot(probs.astype(jnp.bfloat16), g_rows)
            dk = dk + _dot(grad, q_rows)
            dq = _dot(k_turn[rows, span], grad)
            if c == 0:
                dq_turn[rows, cols] = dq
            else:
                dq_turn[rows, cols] += dq

        @pl.when(half == 0)
        def _():
            dk_sum[span, :] = dk
            dv_sum[span, :] = dv

        @pl.when(half == 1)
        def _():
            out_ref[span, wide : 2 * wide] = ((dk_sum[span, :] + dk) * HEAD ** -0.5).astype(jnp.bfloat16)
            out_ref[span, 2 * wide :] = (dv_sum[span, :] + dv).astype(jnp.bfloat16)

    @pl.when(half == 1)
    def _():
        out_ref[:, :wide] = (dq_turn[...] * HEAD ** -0.5).T.astype(jnp.bfloat16)

def attend_backward(slopes, qkv, grad, wide, log, pair, deps=()):
    length = qkv.shape[0]
    spec = lambda part: pl.BlockSpec((length, 2 * HEAD), lambda h: (0, 3 * pair + part))
    return pl.pallas_call(
        backward_kernel,
        grid=(2,),
        in_specs=[
            pl.BlockSpec(memory_space=pltpu.SMEM), spec(0), spec(1), spec(2),
            pl.BlockSpec((length, 2 * HEAD), lambda h: (0, pair)),
            pl.BlockSpec((2 * HEAD, length), lambda h: (0, 0)),
            pl.BlockSpec((8, length), lambda h: (h, 0)),
        ] + [pl.BlockSpec(memory_space=pl.ANY)] * len(deps),
        out_specs=pl.BlockSpec((length, 6 * HEAD), lambda h: (0, 0)),
        out_shape=jax.ShapeDtypeStruct((length, 6 * HEAD), jnp.bfloat16),
        scratch_shapes=[
            pltpu.VMEM((2 * HEAD, length), jnp.bfloat16),
            pltpu.VMEM((2 * HEAD, length), jnp.bfloat16),
            pltpu.VMEM((2 * HEAD, length), jnp.bfloat16),
            pltpu.VMEM((2 * HEAD, length), jnp.float32),
            pltpu.VMEM((length, 2 * HEAD), jnp.float32),
            pltpu.VMEM((length, 2 * HEAD), jnp.float32),
        ],
        compiler_params=pltpu.CompilerParams(vmem_limit_bytes=VMEM_BYTES),
        cost_estimate=estimate(22),
        name="attend_backward",
    )(slopes, qkv, qkv, qkv, grad, wide, log, *deps)

GELU_RATE = math.sqrt(2.0 / math.pi)
GELU_CUBE = 0.044715
CONTRACT_LAST = (((1,), (1,)), ((), ()))


def feed_forward_kernel(groups, per, table_ref, x_ref, g_ref, bias_ref, *refs):
    outs, scratch = refs[-11:-4], refs[-4:]
    chips = table_ref.shape[0] // 2
    down_refs, up_refs = refs[: 2 * groups], refs[2 * groups : -11]
    up_groups = len(up_refs) // 2
    layer_ref, back_ref, down_keep, down_send, up_keep, up_send, bias_out = outs
    x_turn, up_tile, down_tile, grad_tile = scratch
    step = pl.program_id(0)
    core = table_ref[2 * chips]
    steps = chips // (groups * per)
    owned = up_refs[0].shape[1]
    span = down_refs[0].shape[1]

    @pl.when(step == 0)
    def _():
        x_turn[...] = x_ref[...].T
        layer_ref[...] = jnp.zeros_like(layer_ref)
        back_ref[...] = jnp.zeros_like(back_ref)

    def up_rows(place, who):
        start = table_ref[chips + place] * (CORES * owned) + who * owned
        return pl.ds(pl.multiple_of(start, owned), owned)

    for place in range(chips):
        group, at = divmod(place, chips // up_groups)
        up_tile[up_rows(place, core), :] = up_refs[group][at]
        up_tile[up_rows(place, 1 - core), :] = up_refs[up_groups + group][at]

    def down_rows(at, who):
        chip = lax.rem(table_ref[step * per + at], per)
        return pl.ds(pl.multiple_of((chip * CORES + who) * span, span), span)

    for group in range(groups):

        @pl.when(step // steps == group)
        def _():
            for at in range(per):
                down_tile[down_rows(at, core), :] = down_refs[group][at]
                down_tile[down_rows(at, 1 - core), :] = down_refs[groups + group][at]

    upper = _dot(x_ref[...], up_tile[...]) + bias_ref[...]
    square = upper * upper
    turned = jnp.tanh(GELU_RATE * (upper + GELU_CUBE * upper * square))
    lift = 0.5 * (1.0 + turned)
    slope = lift + 0.5 * upper * (1.0 - turned * turned) * (GELU_RATE * (1.0 + 3.0 * GELU_CUBE * square))
    hidden = (upper * lift).astype(jnp.bfloat16)
    grad_upper = lax.dot_general(
        g_ref[...], down_tile[...], CONTRACT_LAST, preferred_element_type=jnp.float32
    ) * slope
    bias_out[...] = jnp.sum(grad_upper, axis=0, keepdims=True)
    upper_low = grad_upper.astype(jnp.bfloat16)
    layer_ref[...] += _dot(hidden, down_tile[...])
    back_ref[...] += lax.dot_general(
        upper_low, up_tile[...], CONTRACT_LAST, preferred_element_type=jnp.float32
    )
    grad_tile[...] = _dot(hidden.T, g_ref[...]).astype(jnp.bfloat16)
    for at in range(per):
        down_keep[at] = grad_tile[down_rows(at, core), :]
        down_send[at] = grad_tile[down_rows(at, 1 - core), :]
    up_tile[...] = _dot(x_turn[...], upper_low).astype(jnp.bfloat16)
    for place in range(chips):
        up_keep[place] = up_tile[up_rows(place, core), :]
        up_send[place] = up_tile[up_rows(place, 1 - core), :]


def group_place(group, size):
    return lambda s, *t: (jnp.clip(s - group * size, 0, size - 1), 0, 0)


def feed_forward(table, x, g, bias, down, up, per=2):
    tokens, width = x.shape
    groups = len(down) // 2
    size, span, _ = down[0].shape
    owned = up[0].shape[1]
    inner = bias.shape[1]
    chips = groups * size
    tile = per * CORES * span
    whole = lambda s, t: (0, 0)
    column = lambda s, t: (0, t[s * per] // per)
    columns = lambda s, t: (0, 0, t[s * per] // per)
    down_spec = lambda place: pl.BlockSpec((per, span, width), place)
    up_spec = lambda count: pl.BlockSpec((count, owned, tile), columns)
    shape = jax.ShapeDtypeStruct
    return pl.pallas_call(
        functools.partial(feed_forward_kernel, groups, per),
        grid_spec=pltpu.PrefetchScalarGridSpec(
            num_scalar_prefetch=1,
            grid=(chips // per,),
            in_specs=[
                pl.BlockSpec((tokens, width), whole),
                pl.BlockSpec((tokens, width), whole),
                pl.BlockSpec((1, tile), column),
            ]
            + [down_spec(group_place(group, size // per)) for group in range(groups)] * 2
            + [up_spec(array.shape[0]) for array in up],
            out_specs=[
                pl.BlockSpec((tokens, width), whole),
                pl.BlockSpec((tokens, width), whole),
                down_spec(lambda s, t: (s, 0, 0)),
                down_spec(lambda s, t: (s, 0, 0)),
                up_spec(chips),
                up_spec(chips),
                pl.BlockSpec((1, tile), column),
            ],
            scratch_shapes=[
                pltpu.VMEM((width, tokens), jnp.bfloat16),
                pltpu.VMEM((width, tile), jnp.bfloat16),
                pltpu.VMEM((tile, width), jnp.bfloat16),
                pltpu.VMEM((tile, width), jnp.bfloat16),
            ],
        ),
        out_shape=[
            shape((tokens, width), jnp.float32),
            shape((tokens, width), jnp.float32),
            shape((chips, span, width), jnp.bfloat16),
            shape((chips, span, width), jnp.bfloat16),
            shape((chips, owned, inner), jnp.bfloat16),
            shape((chips, owned, inner), jnp.bfloat16),
            shape((1, inner), jnp.float32),
        ],
        compiler_params=pltpu.CompilerParams(vmem_limit_bytes=VMEM_BYTES),
        cost_estimate=estimate(45),
        name="feed_forward",
    )(table, x, g, bias, *down, *up)


def bits_of(size):
    return [1 << b for b in range(size.bit_length() - 1)]


def swap(value, step):
    axis, bit = step
    return lax.ppermute(value, axis, [(i, i ^ bit) for i in range(lax.axis_size(axis))])


def other_core(value):
    return swap(value, ("core", 1))


def offsets_of(steps, rings):
    found = [0]
    for axis, bit in steps:
        found = found + [o ^ (bit * rings if axis == "seq" else bit) for o in found]
    return found


def grow(value, steps):
    for step in steps:
        value = jnp.concatenate((value, swap(value, step)), axis=0)
    return value


def after(values, *others):
    values = tuple(values)
    return pl.pallas_call(
        lambda *refs: None,
        in_specs=[pl.BlockSpec(memory_space=pl.ANY)] * (len(values) + len(others)),
        out_specs=[pl.BlockSpec(memory_space=pl.ANY)] * len(values),
        out_shape=[jax.ShapeDtypeStruct(value.shape, value.dtype) for value in values],
        input_output_aliases={i: i for i in range(len(values))},
        name="after",
    )(*values, *others)


def widen(value, step):
    return jnp.stack((value, swap(value, step)), axis=1).reshape((-1,) + value.shape[1:])


def direct(value, axis):
    return [value] + [swap(value, (axis, m)) for m in range(1, lax.axis_size(axis))]


def add_low(left, right):
    return (left.astype(jnp.float32) + right.astype(jnp.float32)).astype(jnp.bfloat16)


def collect(groups, axis):
    total = groups[0].astype(jnp.float32)
    for m in range(1, len(groups)):
        total = total + swap(groups[m], (axis, m)).astype(jnp.float32)
    return total


def fold(total, axis):
    for bit in bits_of(total.shape[0]):
        pairs = total.reshape((total.shape[0] // 2, 2) + total.shape[1:])
        total = pairs[:, 0] + swap(pairs[:, 1].astype(jnp.bfloat16), (axis, bit)).astype(jnp.float32)
    return total[0]


def spread(blocks, axis):
    me = lax.axis_index(axis)
    out = jnp.zeros_like(blocks)
    for m in range(lax.axis_size(axis)):
        block = lax.dynamic_slice_in_dim(blocks, me ^ m, 1, 0)
        came = block if m == 0 else swap(block, (axis, m))
        out = lax.dynamic_update_slice_in_dim(out, came, me ^ m, 0)
    return out


def group_columns(weight, ways):
    rows = weight.shape[0]
    parts = weight.reshape(rows, 3, ways, -1, 2 * HEAD)
    return jnp.transpose(parts, (2, 0, 3, 1, 4)).reshape(ways, rows, -1)


def ungroup_columns(grouped):
    ways, rows, _ = grouped.shape
    parts = grouped.reshape(ways, rows, -1, 3, 2 * HEAD)
    return jnp.transpose(parts, (1, 3, 0, 2, 4)).reshape(rows, -1)


def pair_columns(bias, seq_index, ways):
    parts = bias.reshape(2, ways, -1, 2 * HEAD)
    mine = lax.dynamic_index_in_dim(parts, seq_index, 1, keepdims=False)
    return jnp.stack((mine[0], jnp.zeros_like(mine[0]), mine[1]), axis=1).reshape(-1)


def unpair_columns(sums, seq_index, ways):
    parts = sums.reshape(-1, 3, 2 * HEAD)
    mine = jnp.stack((parts[:, 0], parts[:, 2]))
    out = jnp.zeros((2, ways) + mine.shape[1:], jnp.float32)
    return lax.dynamic_update_slice_in_dim(out, mine[:, None], seq_index, 1).reshape(-1)


def norm_parts(values):
    centre = values - jnp.mean(values, axis=-1, keepdims=True)
    factor = lax.rsqrt(jnp.mean(centre * centre, axis=-1, keepdims=True) + EPSILON)
    return centre * factor, factor


def norm_back(grad, gain, unit, factor):
    turned = grad * gain
    inner = jnp.mean(turned * unit, axis=-1, keepdims=True)
    return factor * (turned - jnp.mean(turned, axis=-1, keepdims=True) - unit * inner)


def project_kernel(ways, table_ref, *refs):
    own_ref, one_ref, two_ref, low_ref, high_ref, w_ref, gain_ref, shift_ref, bias_ref = refs[:9]
    qkv_ref, normed_ref, unit_ref, weight_ref, rows = refs[-5:]
    cut = low_ref.shape[0]
    step = pl.program_id(0)
    copies = w_ref.shape[0]
    owned = weight_ref.shape[0] // (ways * copies)

    @pl.when(step == 0)
    def _():
        for place in range(copies):
            for sender in range(ways):
                start = (sender * copies + (table_ref[1] ^ place)) * owned
                weight_ref[pl.ds(pl.multiple_of(start, owned), owned), :] = w_ref[place, sender, :owned, :]

    for block, ref in enumerate((own_ref, one_ref, two_ref)):

        @pl.when(step == block)
        def _():
            rows[...] = ref[...]

    @pl.when(step == 3)
    def _():
        rows[:cut] = low_ref[...]
        rows[cut:] = high_ref[...]

    unit, _ = norm_parts(rows[...].astype(jnp.float32))
    normed = (unit * gain_ref[...] + shift_ref[...]).astype(jnp.bfloat16)
    unit_ref[...] = unit.astype(jnp.bfloat16)
    normed_ref[...] = normed
    qkv_ref[...] = (_dot(normed, weight_ref[...]) + bias_ref[...]).astype(jnp.bfloat16)


def project(table, blocks, packed, gain, shift, bias, ways, owned, deps=()):
    local, width = blocks[0].shape
    copies, _, _, triple = packed.shape
    whole = lambda s, t: (0, 0)
    place = lambda s, t: (t[0] ^ s, 0)
    full = lambda array: pl.BlockSpec(array.shape, lambda s, t: (0,) * array.ndim)
    operands = tuple(blocks) + (packed, gain, shift, bias)
    shape = jax.ShapeDtypeStruct
    length = ways * local
    return pl.pallas_call(
        functools.partial(project_kernel, ways),
        grid_spec=pltpu.PrefetchScalarGridSpec(
            num_scalar_prefetch=1,
            grid=(ways,),
            in_specs=[full(array) for array in operands]
            + [pl.BlockSpec(memory_space=pl.ANY)] * len(deps),
            out_specs=[
                pl.BlockSpec((local, triple), place),
                pl.BlockSpec((local, width), place),
                pl.BlockSpec((local, width), place),
                pl.BlockSpec((width, triple), whole),
            ],
            scratch_shapes=[pltpu.VMEM((local, width), jnp.bfloat16)],
        ),
        out_shape=[
            shape((length, triple), jnp.bfloat16),
            shape((length, width), jnp.bfloat16),
            shape((length, width), jnp.bfloat16),
            shape((width, triple), jnp.bfloat16),
        ],
        compiler_params=pltpu.CompilerParams(vmem_limit_bytes=VMEM_BYTES),
        cost_estimate=estimate(9),
        name="project",
    )(table, *operands, *deps)


def input_grad_kernel(low_ref, high_ref, w_ref, normed_ref, unit_ref, *refs):
    part_ref, weight_ref, sum_ref, bias_ref, total = refs[-5:]
    step = pl.program_id(0)

    @pl.when(step == 0)
    def _():
        total[...] = jnp.zeros_like(total)
        sum_ref[...] = jnp.zeros_like(sum_ref)
        bias_ref[...] = jnp.zeros_like(bias_ref)

    grad = jnp.concatenate((low_ref[...], high_ref[...]), axis=1)
    part = lax.dot_general(grad, w_ref[...], CONTRACT_LAST, preferred_element_type=jnp.float32)
    part_ref[...] = part.astype(jnp.bfloat16)
    total[...] += _dot(normed_ref[...].T, grad)
    sum_ref[0:1] += jnp.sum(part * unit_ref[...].astype(jnp.float32), axis=0, keepdims=True)
    sum_ref[1:2] += jnp.sum(part, axis=0, keepdims=True)
    bias_ref[0:1] += jnp.sum(grad.astype(jnp.float32), axis=0, keepdims=True)

    @pl.when(step == pl.num_programs(0) - 1)
    def _():
        weight_ref[...] = total[...].astype(jnp.bfloat16)


def input_grad(low, high, weight, normed, unit, deps=()):
    length, width = normed.shape
    triple = weight.shape[1]
    rows = 512
    block = lambda columns: pl.BlockSpec((rows, columns), lambda s: (s, 0))
    whole = lambda *size: pl.BlockSpec(size, lambda s: (0, 0))
    shape = jax.ShapeDtypeStruct
    return pl.pallas_call(
        input_grad_kernel,
        grid=(length // rows,),
        in_specs=[block(triple // 2), block(triple // 2), whole(width, triple), block(width), block(width)]
        + [pl.BlockSpec(memory_space=pl.ANY)] * len(deps),
        out_specs=[block(width), whole(width, triple), whole(8, width), whole(8, triple)],
        out_shape=[
            shape((length, width), jnp.bfloat16),
            shape((width, triple), jnp.bfloat16),
            shape((8, width), jnp.float32),
            shape((8, triple), jnp.float32),
        ],
        scratch_shapes=[pltpu.VMEM((width, triple), jnp.float32)],
        compiler_params=pltpu.CompilerParams(vmem_limit_bytes=VMEM_BYTES),
        cost_estimate=estimate(10),
        name="input_grad",
    )(low, high, weight, normed, unit, *deps)


def output_rows(table_ref, place, who, owned):
    start = table_ref[place] * (CORES * owned) + who * owned
    return pl.ds(pl.multiple_of(start, owned), owned)


def join_groups(ref):
    return jnp.concatenate([ref[s] for s in range(ref.shape[0])], axis=1)


def output_kernel(table_ref, context_ref, x_ref, bias_ref, gain_ref, shift_ref, *refs):
    residual_ref, normed_ref, weight_ref = refs[-3:]
    parts = refs[:-3]
    groups = len(parts) // 2
    size, owned, _ = parts[0].shape
    core = table_ref[2 * groups * size]

    @pl.when(pl.program_id(0) == 0)
    def _():
        for place in range(groups * size):
            group, at = divmod(place, size)
            weight_ref[output_rows(table_ref, groups * size + place, core, owned), :] = parts[group][at]
            weight_ref[output_rows(table_ref, groups * size + place, 1 - core, owned), :] = parts[groups + group][at]

    branch = _dot(join_groups(context_ref), weight_ref[...]) + bias_ref[...]
    residual = x_ref[...].astype(jnp.float32) + branch
    residual_ref[...] = residual
    unit, _ = norm_parts(residual)
    normed_ref[...] = (unit * gain_ref[...] + shift_ref[...]).astype(jnp.bfloat16)


def project_output(table, context, parts, x, bias, gain, shift):
    local, width = x.shape
    ways = context.shape[0]
    rows = 256
    vector = pl.BlockSpec((1, width), lambda s, t: (0, 0))
    block = pl.BlockSpec((rows, width), lambda s, t: (s, 0))
    heads = pl.BlockSpec((ways, rows, width // ways), lambda s, t: (0, s, 0))
    size, owned, total = parts[0].shape
    weight = pl.BlockSpec((size, owned, width), lambda s, t: (0, 0, total // width - 1))
    shape = jax.ShapeDtypeStruct
    return pl.pallas_call(
        output_kernel,
        grid_spec=pltpu.PrefetchScalarGridSpec(
            num_scalar_prefetch=1,
            grid=(local // rows,),
            in_specs=[heads, block, vector, vector, vector] + [weight] * len(parts),
            out_specs=[block, block, pl.BlockSpec((width, width), lambda s, t: (0, 0))],
        ),
        out_shape=[
            shape((local, width), jnp.float32),
            shape((local, width), jnp.bfloat16),
            shape((width, width), jnp.bfloat16),
        ],
        compiler_params=pltpu.CompilerParams(vmem_limit_bytes=VMEM_BYTES),
        cost_estimate=estimate(5),
        name="project_output",
    )(table, context, x, bias, gain, shift, *parts)


def residual_kernel(table_ref, grad_ref, residual_ref, up_ref, context_ref, w_ref, gain_ref, *refs):
    out_ref, context_grad_ref, keep_ref, send_ref, sum_ref, total, held = refs[-7:]
    step = pl.program_id(0)
    chips, owned, _ = keep_ref.shape
    ways = context_ref.shape[0]
    core = table_ref[2 * chips]

    @pl.when(step == 0)
    def _():
        total[...] = jnp.zeros_like(total)
        sum_ref[...] = jnp.zeros_like(sum_ref)

    unit, factor = norm_parts(residual_ref[...])
    grad = grad_ref[...]
    upstream = up_ref[...].astype(jnp.float32)
    through = upstream + norm_back(grad, gain_ref[...], unit, factor)
    out_ref[...] = through
    branch = through.astype(jnp.bfloat16)
    context_grad = lax.dot_general(
        branch, w_ref[...], CONTRACT_LAST, preferred_element_type=jnp.float32
    ).astype(jnp.bfloat16)
    wide = context_grad.shape[1] // ways
    for s in range(ways):
        context_grad_ref[s] = context_grad[:, s * wide : (s + 1) * wide]
    total[...] += _dot(join_groups(context_ref).T, branch)
    for row, term in enumerate((grad * unit, grad, through, upstream)):
        sum_ref[row : row + 1] += jnp.sum(term, axis=0, keepdims=True)

    @pl.when(step == pl.num_programs(0) - 1)
    def _():
        held[...] = total[...].astype(jnp.bfloat16)
        for place in range(chips):
            keep_ref[place] = held[output_rows(table_ref, place, core, owned), :]
            send_ref[place] = held[output_rows(table_ref, place, 1 - core, owned), :]


def residual_grad(table, grad, residual, upstream, context, weight, gain, chips):
    local, width = residual.shape
    ways = context.shape[0]
    rows = 256
    owned = width // (chips * CORES)
    whole = lambda *size: pl.BlockSpec(size, lambda s, t: (0,) * len(size))
    block = pl.BlockSpec((rows, width), lambda s, t: (s, 0))
    heads = pl.BlockSpec((ways, rows, width // ways), lambda s, t: (0, s, 0))
    shape = jax.ShapeDtypeStruct
    return pl.pallas_call(
        residual_kernel,
        grid_spec=pltpu.PrefetchScalarGridSpec(
            num_scalar_prefetch=1,
            grid=(local // rows,),
            in_specs=[block, block, block, heads, whole(width, width), whole(1, width)],
            out_specs=[block, heads, whole(chips, owned, width), whole(chips, owned, width), whole(8, width)],
            scratch_shapes=[pltpu.VMEM((width, width), jnp.float32), pltpu.VMEM((width, width), jnp.bfloat16)],
        ),
        out_shape=[
            shape((local, width), jnp.float32),
            shape((ways, local, width // ways), jnp.bfloat16),
            shape((chips, owned, width), jnp.bfloat16),
            shape((chips, owned, width), jnp.bfloat16),
            shape((8, width), jnp.float32),
        ],
        compiler_params=pltpu.CompilerParams(vmem_limit_bytes=VMEM_BYTES),
        cost_estimate=estimate(7),
        name="residual_grad",
    )(table, grad, residual, upstream, context, weight, gain)


def meet_kernel(groups, up_groups, down_keep, down_came, output_keep, output_came, up_keep, up_came, *refs):
    step = pl.program_id(0)
    steps = pl.num_programs(0)
    span = down_keep.shape[1]

    def both(left, right):
        return (left[...].astype(jnp.float32) + right[...].astype(jnp.float32)).astype(jnp.bfloat16)

    for group in range(groups):

        @pl.when(step // (steps // groups) == group)
        def _():
            refs[group][:, :span] = both(down_keep, down_came)
            refs[group][:, span:] = both(output_keep, output_came)

    for group in range(up_groups):

        @pl.when(step // (steps // up_groups) == group)
        def _():
            refs[groups + group][...] = both(up_keep, up_came)


def meet(down_keep, down_came, output_keep, output_came, up_keep, up_came, groups, up_groups, per=4):
    chips, span, width = down_keep.shape
    owned, inner = up_keep.shape[1:]
    block = lambda rows, columns: pl.BlockSpec((per, rows, columns), lambda s: (s, 0, 0))
    parts = [(span + owned, width, chips // groups, group) for group in range(groups)]
    parts += [(owned, inner, chips // up_groups, group) for group in range(up_groups)]
    outs = [pl.BlockSpec((per, rows, columns), group_place(group, size // per)) for rows, columns, size, group in parts]
    shapes = [jax.ShapeDtypeStruct((size, rows, columns), jnp.bfloat16) for rows, columns, size, _ in parts]
    return pl.pallas_call(
        functools.partial(meet_kernel, groups, up_groups),
        grid=(chips // per,),
        in_specs=[block(span, width)] * 2 + [block(owned, width)] * 2 + [block(owned, inner)] * 2,
        out_specs=outs,
        out_shape=shapes,
        compiler_params=pltpu.CompilerParams(vmem_limit_bytes=VMEM_BYTES),
        cost_estimate=estimate(9),
        name="meet",
    )(down_keep, down_came, output_keep, output_came, up_keep, up_came)


def halve(value, step, kind):
    axis, bit = step
    mine = (lax.axis_index(axis) // bit) % 2
    sent = lax.dynamic_index_in_dim(value, 1 - mine, 0, keepdims=False).astype(kind)
    kept = lax.dynamic_index_in_dim(value, mine, 0, keepdims=False)
    return kept.astype(jnp.float32) + swap(sent, step).astype(jnp.float32)


def scatter_copies(value, kind):
    rings = lax.axis_size("ring")
    value = jnp.moveaxis(value.reshape((rings, CORES) + value.shape[1:]), 1, 0)
    value = halve(value, ("core", 1), kind)
    for bit in bits_of(rings):
        shape = value.shape
        value = jnp.moveaxis(value.reshape((shape[0] // 2, 2) + shape[1:]), 1, 0)
        value = halve(value, ("ring", bit), kind)
    return value[0]


def scatter_seq(value, kind):
    for bit in reversed(bits_of(lax.axis_size("seq"))):
        value = halve(value.reshape((2, value.shape[0] // 2) + value.shape[1:]), ("seq", bit), kind)
    return value[0]


def layer_norm(values, norm_gain, norm_shift):
    centre = values - jnp.mean(values, axis=-1, keepdims=True)
    spread = jnp.mean(centre * centre, axis=-1, keepdims=True)
    return centre * lax.rsqrt(spread + EPSILON) * norm_gain + norm_shift


def tanh_gelu(upper_in):
    return jax.nn.gelu(upper_in, approximate=True)


def gather_small(parts):
    sizes = [part.shape[0] for part in parts]
    width = -(-sum(sizes) // 512) * 512
    packed = jnp.concatenate(list(parts) + [jnp.zeros((width - sum(sizes),), parts[0].dtype)])
    whole = lax.all_gather(packed.reshape(4, width // 4), WORLD, axis=0, tiled=False)
    whole = whole.reshape(-1, width).astype(jnp.float32)
    out, start = [], 0
    for size in sizes:
        out.append(whole[:, start : start + size].reshape(-1))
        start += size
    return out


def scatter_small(parts, world):
    rows = [part.reshape(world, -1) for part in parts]
    sizes = [row.shape[1] for row in rows]
    width = -(-sum(sizes) // 128) * 128
    packed = jnp.concatenate(rows + [jnp.zeros((world, width - sum(sizes)), jnp.float32)], axis=1)
    owned = lax.psum_scatter(packed, WORLD, scatter_dimension=0, tiled=True)[0]
    out, start = [], 0
    for size in sizes:
        out.append(owned[start : start + size])
        start += size
    return out


def gather_weight(shard):
    mine = lax.all_gather(shard, CHIPS, axis=0, tiled=False)
    theirs = other_core(mine)
    first = lax.axis_index("core") == 0
    pair = jnp.stack((jnp.where(first, mine, theirs), jnp.where(first, theirs, mine)), axis=1)
    return pair.reshape(-1, shard.shape[-1])


def pick_rows(columns, chips, core):
    tokens, width = columns.shape
    parts = columns.reshape(tokens, chips, CORES, width // (chips * CORES))
    return lax.dynamic_index_in_dim(parts, core, 2, keepdims=False).reshape(tokens, width // CORES)


def contract_tokens(left, right):
    return lax.dot_general(left, right, (((0,), (0,)), ((), ())), preferred_element_type=jnp.float32)


def scatter_weight_grad(left, right, chips):
    core = lax.axis_index("core")
    sent = contract_tokens(pick_rows(left, chips, 1 - core), right).astype(jnp.bfloat16)
    came = other_core(sent).astype(jnp.float32)
    both = (contract_tokens(pick_rows(left, chips, core), right) + came).astype(jnp.bfloat16)
    return lax.psum_scatter(both, CHIPS, scatter_dimension=0, tiled=True).astype(jnp.float32)


def plain_body(
    tokens_in,
    out_grad,
    first_gain,
    first_shift,
    input_weight,
    input_bias,
    output_weight,
    output_bias,
    second_gain,
    second_shift,
    up_weight,
    up_bias,
    down_weight,
    down_bias,
):
    ways = lax.axis_size("seq")
    rings = lax.axis_size("ring")
    chips = ways * rings
    model_width = tokens_in.shape[-1]
    group_width = model_width // ways
    head_group = group_width // HEAD
    rows_in = tokens_in.reshape(-1, model_width)
    local = rows_in.shape[0]
    length = local * ways
    upstream = out_grad.reshape(local, model_width)

    (
        gain_first,
        shift_first,
        bias_input,
        bias_output,
        gain_second,
        shift_second,
        bias_up,
        bias_down,
    ) = gather_small(
        (first_gain, first_shift, input_bias, output_bias, second_gain, second_shift, up_bias, down_bias)
    )
    seq_index = lax.axis_index("seq")

    all_rows = lax.all_gather(rows_in, "seq", axis=0, tiled=True)
    owned_rows = input_weight.shape[0]
    by_group = group_columns(input_weight, ways)
    columns = lax.all_to_all(by_group, "seq", split_axis=0, concat_axis=0, tiled=True)
    columns = lax.all_gather(columns, ("ring", "core"), axis=0, tiled=False)
    weight_input = jnp.moveaxis(columns, 0, 1).reshape(model_width, 3 * group_width)

    weight_output = gather_weight(output_weight)
    weight_up = gather_weight(up_weight)
    weight_down = gather_weight(down_weight)

    normed = layer_norm(all_rows.astype(jnp.float32), gain_first, shift_first).astype(jnp.bfloat16)
    bias_group = pair_columns(bias_input, seq_index, ways)
    qkv = (jnp.dot(normed, weight_input, preferred_element_type=jnp.float32) + bias_group).astype(
        jnp.bfloat16
    )
    head_ids = (seq_index * head_group + jnp.arange(head_group, dtype=jnp.int32)).astype(jnp.float32)
    slopes = jnp.exp2(-8.0 * (head_ids + 1.0) / HEADS)
    pairs = range(head_group // 2)
    kept = [attend_forward(slopes[2 * p : 2 * p + 2], qkv, p) for p in pairs]
    context_split = jnp.concatenate([k[0] for k in kept], axis=1)
    context = lax.all_to_all(
        context_split.reshape(ways, local, group_width), "seq", split_axis=0, concat_axis=0, tiled=True
    )
    context = jnp.moveaxis(context, 0, 1).reshape(local, model_width)

    inputs = rows_in.astype(jnp.float32)
    branch = jnp.dot(context, weight_output, preferred_element_type=jnp.float32) + bias_output
    residual = inputs + branch
    normed_two_float, second_back = jax.vjp(layer_norm, residual, gain_second, shift_second)
    normed_two = normed_two_float.astype(jnp.bfloat16)
    upper = jnp.dot(normed_two, weight_up, preferred_element_type=jnp.float32) + bias_up
    activated, gelu_back = jax.vjp(tanh_gelu, upper)
    hidden = activated.astype(jnp.bfloat16)
    layer_out = (
        residual + jnp.dot(hidden, weight_down, preferred_element_type=jnp.float32) + bias_down
    ).astype(jnp.bfloat16)
    grad_hidden = lax.dot_general(
        upstream, weight_down, (((1,), (1,)), ((), ())), preferred_element_type=jnp.float32
    )
    grad_upper = gelu_back(grad_hidden)[0]
    upper_low = grad_upper.astype(jnp.bfloat16)
    grad_normed_two = lax.dot_general(
        upper_low, weight_up, (((1,), (1,)), ((), ())), preferred_element_type=jnp.float32
    )
    grad_through, grad_second_gain, grad_second_shift = second_back(grad_normed_two)
    grad_residual = upstream.astype(jnp.float32) + grad_through
    branch_low = grad_residual.astype(jnp.bfloat16)
    context_grad = lax.dot_general(
        branch_low, weight_output, (((1,), (1,)), ((), ())), preferred_element_type=jnp.float32
    ).astype(jnp.bfloat16)
    grad_split = jnp.moveaxis(context_grad.reshape(local, ways, group_width), 1, 0)
    grad_split = lax.all_to_all(grad_split, "seq", split_axis=0, concat_axis=0, tiled=True)
    grad_split = grad_split.reshape(length, group_width)

    grad_down_weight = scatter_weight_grad(hidden, upstream, chips)
    grad_up_weight = scatter_weight_grad(normed_two, upper_low, chips)
    grad_output_weight = scatter_weight_grad(context, branch_low, chips)

    grad_qkv = jnp.concatenate(
        [
            attend_backward(
                slopes[2 * p : 2 * p + 2], qkv, grad_split, kept[p][1], kept[p][2], p
            )
            for p in pairs
        ],
        axis=1,
    )

    grad_normed = lax.dot_general(
        grad_qkv, weight_input, (((1,), (1,)), ((), ())), preferred_element_type=jnp.float32
    ).astype(jnp.bfloat16)
    grad_normed = lax.all_to_all(
        grad_normed.reshape(ways, local, model_width), "seq", split_axis=0, concat_axis=0, tiled=True
    )
    grad_normed = jnp.sum(grad_normed.astype(jnp.float32), axis=0)

    grad_columns = contract_tokens(normed, grad_qkv)
    grad_columns = jnp.moveaxis(
        grad_columns.reshape(ways, rings * CORES, owned_rows, 3 * group_width), 1, 0
    ).astype(jnp.bfloat16)
    grad_columns = lax.psum_scatter(
        grad_columns.reshape(-1, 3 * group_width), ("ring", "core"), scatter_dimension=0, tiled=True
    )
    grad_columns = lax.all_to_all(
        grad_columns.reshape(ways, owned_rows, 3 * group_width), "seq", split_axis=0, concat_axis=0, tiled=True
    )
    grad_input_weight = ungroup_columns(grad_columns).astype(jnp.float32)
    grad_input_bias = unpair_columns(jnp.sum(grad_qkv.astype(jnp.float32), axis=0), seq_index, ways)
    _, first_back = jax.vjp(layer_norm, inputs, gain_first, shift_first)
    grad_entry, grad_first_gain, grad_first_shift = first_back(grad_normed)
    tokens_grad = grad_residual + grad_entry

    small = scatter_small(
        (
            grad_first_gain,
            grad_first_shift,
            grad_input_bias,
            jnp.sum(grad_residual, axis=0),
            grad_second_gain,
            grad_second_shift,
            jnp.sum(grad_upper, axis=0),
            jnp.sum(upstream.astype(jnp.float32), axis=0),
        ),
        chips * CORES,
    )
    return (
        layer_out.reshape(tokens_in.shape),
        tokens_grad.reshape(tokens_in.shape),
        small[0],
        small[1],
        grad_input_weight,
        small[2],
        grad_output_weight,
        small[3],
        small[4],
        small[5],
        grad_up_weight,
        small[6],
        grad_down_weight,
        small[7],
    )


def blocked_body(
    tokens_in,
    out_grad,
    first_gain,
    first_shift,
    input_weight,
    input_bias,
    output_weight,
    output_bias,
    second_gain,
    second_shift,
    up_weight,
    up_bias,
    down_weight,
    down_bias,
):
    ways = lax.axis_size("seq")
    rings = lax.axis_size("ring")
    chips = ways * rings
    copies = rings * CORES
    world = chips * CORES
    model_width = tokens_in.shape[-1]
    head_group = model_width // ways // HEAD
    rows_in = tokens_in.reshape(-1, model_width)
    local = rows_in.shape[0]
    length = local * ways
    upstream = out_grad.reshape(local, model_width)
    seq_index = lax.axis_index("seq")
    core = lax.axis_index("core")
    chip_index = seq_index * rings + lax.axis_index("ring")
    copy_index = lax.axis_index("ring") * CORES + core

    ring = lax.axis_index("ring")
    far_bit, near_bit = rings // 2, 1
    down_away = [s * rings + r for s in range(ways) for r in range(rings)]
    up_away = [s * rings + near + far for near in (0, near_bit) for s in range(ways) for far in (0, far_bit)]
    down_table, up_table = (jnp.array(away, jnp.int32) ^ chip_index for away in (down_away, up_away))
    table = jnp.concatenate((down_table, up_table, core[None]))

    vectors = (first_gain, first_shift, input_bias, output_bias, second_gain, second_shift, up_bias, down_bias)
    sizes = [vector.shape[0] for vector in vectors]
    owned = input_weight.shape[0]
    by_group = group_columns(input_weight, ways)
    triple = by_group.shape[-1]
    packed = jnp.concatenate([jnp.pad(vector, (0, 128 - vector.shape[0]))[None] for vector in vectors])
    packed = jnp.pad(packed, ((0, 8 - len(sizes)), (0, triple - 128)))
    by_group = jnp.concatenate((by_group, jnp.broadcast_to(packed[None], (ways, 8, triple))), axis=1)
    up_shard = jnp.concatenate((up_weight, output_weight), axis=1)
    seq_steps = [("seq", bit) for bit in bits_of(ways)]
    one, two = (swap(rows_in, step) for step in seq_steps)
    up_one = widen(up_shard[None], ("ring", far_bit))
    (by_group,) = after((by_group,), up_one)
    (grouped,) = after((spread(by_group, "seq"),), one, two)
    cut = local // 2
    low, high = swap(two[:cut], seq_steps[0]), swap(one[cut:], seq_steps[1])
    blocks = (rows_in, one, two, low, high)
    columns = grouped[None]
    for bit in (far_bit, near_bit):
        columns = widen(columns, ("ring", bit))
        if bit == far_bit:
            (columns,) = after((columns,), low, high)
            (down_one,) = after((down_weight[None],), columns)
    for bit in (far_bit, near_bit):
        down_one = widen(down_one, ("ring", bit))
    columns = jnp.stack((columns, other_core(columns)), axis=1).reshape((copies,) + by_group.shape)
    found = columns[:, :, owned : owned + len(sizes), :128].reshape(world, -1)
    here = jnp.arange(world, dtype=jnp.int32)
    wanted = ((here % copies) ^ copy_index) * ways + here // copies
    pick = (wanted[:, None] == here[None, :]).astype(jnp.bfloat16)
    found = jnp.dot(pick, found, preferred_element_type=jnp.float32)
    vectors = [found[:, 128 * i : 128 * i + size].reshape(1, -1) for i, size in enumerate(sizes)]
    gain_first, shift_first, bias_input, bias_output, gain_second, shift_second, bias_up, bias_down = vectors
    bias_group = pair_columns(bias_input[0], seq_index, ways)[None]


    (up_one,) = after((up_one,), low, high)
    up_near = jnp.concatenate(direct(up_one, "seq"))
    (down_one,) = after((down_one,), up_near)
    (up_near,) = after((up_near,), columns, down_one)
    down_mine = direct(down_one, "seq")
    up_far = swap(up_near, ("ring", near_bit))

    places = jnp.stack((seq_index, copy_index)).astype(jnp.int32)
    qkv, normed, unit, weight_input = project(
        places, blocks, columns, gain_first, shift_first, bias_group, ways, owned
    )
    head_ids = (seq_index * head_group + jnp.arange(head_group, dtype=jnp.int32)).astype(jnp.float32)
    slopes = jnp.exp2(-8.0 * (head_ids + 1.0) / HEADS)

    def exchange(value):
        return lax.all_to_all(
            value.reshape(ways, local, -1), "seq", split_axis=0, concat_axis=0, tiled=True
        )

    swapped = other_core(up_near)
    kept, contexts, done = [], [], (down_one, up_near)
    for pair in range(2):
        context, wide, log_totals = attend_forward(slopes[2 * pair : 2 * pair + 2], qkv, pair, done)
        kept.append((wide, log_totals))
        contexts.append(context)
        done = (log_totals, swapped)
    context = exchange(jnp.concatenate(contexts, axis=1))

    late = list(after([up_far] + down_mine, context))
    theirs = [other_core(group) for group in late]
    down = late[1:] + theirs[1:]
    up = [up_near, late[0], swapped, theirs[0]]
    residual, normed_two, weight_output = project_output(
        table, context, up, rows_in, bias_output, gain_second, shift_second
    )
    layer, grad_normed_two, down_keep, down_send, up_keep, up_send, grad_up_bias = feed_forward(
        table, normed_two, upstream, bias_up, down, up
    )
    grad_residual, context_grad, output_keep, output_send, middle_sums = residual_grad(
        table, grad_normed_two, residual, upstream, context, weight_output, gain_second, chips
    )

    context_grad = exchange(context_grad).reshape(length, -1)
    met = list(
        meet(down_keep, other_core(down_send), output_keep, other_core(output_send), up_keep, other_core(up_send), ways, 2)
    )
    met = list(after(met, context_grad))
    came = [swap(met[m], ("seq", m)) for m in range(1, ways)] + [swap(met[ways + 1], ("ring", near_bit))]

    grads, ready = [], [met[0], met[ways]]
    for pair in range(2):
        grads.append(attend_backward(slopes[2 * pair : 2 * pair + 2], qkv, context_grad, *kept[pair], pair, ready))
        ready = [grads[0]]
    (up_came,) = after(came[ways - 1 :], grads[1])
    up_sum = (met[ways].astype(jnp.float32) + up_came.astype(jnp.float32)).astype(jnp.bfloat16)
    up_sum = up_sum.reshape((ways, 2) + up_sum.shape[1:])
    down_sum = met[0].astype(jnp.float32)
    for group in after(came[: ways - 1], up_sum):
        down_sum = down_sum + group.astype(jnp.float32)

    part, grad_columns, first_sums, bias_sums = input_grad(
        grads[0], grads[1], weight_input, normed, unit, (down_sum, up_sum)
    )
    up_came = [swap(up_sum[m], ("seq", m)) for m in range(1, ways)]
    down_sum = down_sum.reshape((2, 2) + down_sum.shape[1:])
    down_came = swap(down_sum[:, 1].astype(jnp.bfloat16), ("ring", near_bit))
    down_sum = down_sum[:, 0] + down_came.astype(jnp.float32)
    sums = (
        first_sums[0],
        first_sums[1],
        unpair_columns(bias_sums[0], seq_index, ways),
        middle_sums[2],
        middle_sums[0],
        middle_sums[1],
        grad_up_bias[0],
        middle_sums[3],
    )
    rows = [jnp.pad(term.reshape(world, -1), ((0, 0), (0, 128 - size))) for term, size in zip(sums, sizes)]
    rows = jnp.stack(rows, axis=1).astype(jnp.bfloat16)
    rows = jnp.pad(rows, ((0, 0), (0, 8 - len(sizes)), (0, triple - 128)))
    both = jnp.concatenate((grad_columns.reshape(world, owned, triple), rows), axis=1)
    both = both.reshape(ways, rings, CORES, owned + 8, triple)
    came = other_core(lax.dynamic_index_in_dim(both, 1 - core, 2, keepdims=False))
    (came,) = after((came,), *up_came, down_came)
    both = lax.dynamic_index_in_dim(both, core, 2, keepdims=False).astype(jnp.float32) + came.astype(jnp.float32)
    ring = lax.axis_index("ring")
    both = jnp.stack([lax.dynamic_index_in_dim(both, ring ^ m, 1, keepdims=False) for m in range(rings)])
    up_sum = up_sum[0].astype(jnp.float32)
    for group in up_came:
        up_sum = up_sum + group.astype(jnp.float32)
    grad_normed = jnp.sum(exchange(part).astype(jnp.float32), axis=0)
    inputs = rows_in.astype(jnp.float32)
    tokens_grad = grad_residual + norm_back(grad_normed, gain_first, *norm_parts(inputs))

    (layer,) = after((layer,), both)
    layer_out = (residual + layer + bias_down).astype(jnp.bfloat16)
    both = fold(both, "ring").astype(jnp.bfloat16)
    down_low, up_low = after([value[1].astype(jnp.bfloat16) for value in (down_sum, up_sum)], both)
    down_came, up_came = swap(down_low, ("ring", far_bit)), swap(up_low, ("ring", far_bit))
    both = spread(both, "seq")
    down_came, up_came = after((down_came, up_came), tokens_grad)
    down_sum = down_sum[0] + down_came.astype(jnp.float32)
    grad_up_weight = up_sum[0] + up_came.astype(jnp.float32)
    grad_down_weight, grad_output_weight = down_sum[: down_weight.shape[0]], down_sum[down_weight.shape[0] :]
    wide = 2 * HEAD
    grad_input_weight = jnp.concatenate(
        [
            both[sender, :owned, (3 * pair + part) * wide : (3 * pair + part + 1) * wide]
            for part in range(3)
            for sender in range(ways)
            for pair in range(head_group // 2)
        ],
        axis=1,
    ).astype(jnp.float32)
    rows = jnp.sum(both[:, owned:, :128].astype(jnp.float32), axis=0)
    small = [rows[i, :size] for i, size in enumerate(sizes)]
    return (
        layer_out.reshape(tokens_in.shape),
        tokens_grad.reshape(tokens_in.shape),
        small[0],
        small[1],
        grad_input_weight,
        small[2],
        grad_output_weight,
        small[3],
        small[4],
        small[5],
        grad_up_weight,
        small[6],
        grad_down_weight,
        small[7],
    )


def solution(mesh):
    ways, copies = mesh.shape["seq"], mesh.shape["dp"]
    split = Mesh(mesh.devices.reshape(ways, copies // CORES, CORES), WORLD)
    token = P(("ring", "core"), "seq", None)
    vector = P(WORLD)
    matrix = P(WORLD, None)
    weights = (vector, vector, matrix, vector, matrix, vector, vector, vector, matrix, vector, matrix, vector)
    step = blocked_body if ways == 4 else plain_body
    return jax.shard_map(
        step,
        mesh=split,
        in_specs=(token, token) + weights,
        out_specs=(token, token) + weights,
        check_vma=False,
    )
```
